32 devices in a mesh: dp: 2 (over x), tensor: 16 (over z, y, core).
Axes of the slice: x: 2, y: 2, z: 4, core: 2. Of those that a mesh axis runs over, the one named last changes fastest.
Arguments:
- tokens: bfloat16 [8192, 1536], P(('dp', 'tensor')), may hold values from -6 to 6
- lengths: int32 [2], P('dp'), may hold values from 256 to 4096
- routes: int32 [8192, 8], P(('dp', 'tensor')), may hold values from 0 to 15, all different within a row; in each aligned block of 256 rows (0 to 255, 256 to 511, ...) at most 160 rows name the same one
- norm_gain: float32 [1536], replicated, may hold values from 0.1 to 1.9
- router: bfloat16 [1536, 16], replicated, may hold values from -0.15625 to 0.15625
- w_gate: bfloat16 [16, 1536, 512], P('tensor', 'dp'), may hold values from -0.15625 to 0.15625
- w_up: bfloat16 [16, 1536, 512], P('tensor', 'dp'), may hold values from -0.15625 to 0.15625
- w_down: bfloat16 [16, 512, 1536], P('tensor', None, 'dp'), may hold values from -0.25 to 0.25
Outputs:
- mixed: bfloat16 [8192, 1536], P(('dp', 'tensor'))
The draws below stay inside these ranges and needn't reach their ends.
Inputs may be any that keep to these rules, and one draw needn't show every extreme that they name: `routes`: each row names 8 different experts; among the 256 rows of one device (aligned blocks) no expert is named more than 160 times, and in some device one expert is named exactly 160 times.
All inputs are finite; a program needn't handle non-finite values.
Results may differ from the reference program's by a relative error of at most 0.0048.
Values may be sent and summed in bfloat16 or wider, within the bound.
No kernel may reach another device: no remote copies, remote signals or barrier semaphores. Data moves between devices by JAX's collectives and lax.ppermute only.
A program may use at most 64 MiB of HBM per device.

```python
import math
import jax
import jax.numpy as jnp
import numpy as np
from jax import lax

D = 1536
HID = 512
TOP = 8
LMAX = 4096
EXPERTS = 16
TOK_DEV = 256
TOKENS = 8192
REQS = 2
CAP = 160
N_DP = 2
N_TENSOR = 16


def level_of(key, dims, pieces, smallest, largest):
    factor_of = 1.0
    for axis_at, parts in pieces:
        draws = jax.random.uniform(jax.random.fold_in(jax.random.fold_in(key, 6), axis_at), (parts,), jnp.float32, smallest / len(pieces), largest / len(pieces))
        factor_of = factor_of * jnp.repeat(jnp.exp(draws), dims[axis_at] // parts).reshape((-1,) + (1,) * (len(dims) - 1 - axis_at))
    return factor_of


def shared_out(own_key, own, number, rows, amount, top, limit, skew):
    sequence = jax.random.permutation(own_key, amount)
    packed, common = portions_of(amount, rows * top, limit, skew, True), portions_of(amount, rows * top, limit, skew, False)
    places = jnp.arange(amount)

    def named(sizes, rotation):
        used = int((sizes > 0).sum())
        fixed = max(1, used // 4)
        shifted = fixed + (places - fixed + rotation * (used - fixed)) % max(1, amount - fixed)
        return jnp.zeros((amount,), jnp.int32).at[sequence[jnp.where(places < fixed, places, shifted)]].set(jnp.asarray(sizes, jnp.int32))

    sizes = jnp.where(number % 4 == 0, named(packed, number // 4), named(common, number - number // 4 - 1))
    mixed = jax.random.permutation(jax.random.fold_in(own, 3), amount)
    donor, sink = mixed[0:amount // 2 * 2:2], mixed[1:amount // 2 * 2:2]
    margin = jnp.minimum(sizes[donor] - 1, limit - sizes[sink]) // 2
    margin = jnp.where((donor == sequence[0]) | (sink == sequence[0]) | (sizes[sink] == 0), 0, jnp.maximum(margin, 0))
    shifted = jax.random.randint(jax.random.fold_in(own, 4), (amount // 2,), 0, 1 << 20) % (margin + 1)
    sizes = sizes.at[donor].add(-shifted).at[sink].add(shifted)
    items = jnp.searchsorted(jnp.cumsum(sizes), jnp.arange(rows * top), side="right").astype(jnp.int32)
    listing = items.reshape(top, rows).T
    listing = listing[jax.random.permutation(jax.random.fold_in(own, 1), rows)]
    rotation = jax.random.randint(jax.random.fold_in(own, 2), (rows, 1), 0, top)
    return jnp.take_along_axis(listing, (jnp.arange(top)[None, :] + rotation) % top, axis=1)


def portions_of(number_of, total, bound, slope, full):
    portions = [(1 << 20) // math.isqrt(rank ** slope) + 1 for rank in range(1, number_of + 1)]
    largest = bound if full else min(bound, max(-(-total // number_of), total * portions[0] // sum(portions)))
    least = 1 if total - largest >= number_of - 1 else 0
    given, surplus = [largest] + [least] * (number_of - 1), total - largest - least * (number_of - 1)
    while surplus > 0:
        movable = [i for i in range(1, number_of) if given[i] < largest] or [i for i in range(1, number_of) if given[i] < bound]
        pool, left = sum([portions[i] for i in movable]), surplus
        for i in movable:
            addition = min(bound - given[i], max(1, left * portions[i] // pool), surplus)
            given[i] = given[i] + addition
            surplus = surplus - addition
    return np.array(given)


def normal_values(own_key, extent, spread, bound, split=(), kind=jnp.bfloat16):
    level = level_of(own_key, extent, split, -0.22, 0.18) if split else 1.0
    drawn = jax.random.normal(own_key, extent, jnp.float32) * spread * level
    return jnp.minimum(jnp.maximum(drawn, -bound), bound).astype(kind)


def setup_inputs(seed: int = 0) -> dict:
    splits = jax.random.split(jax.random.key(seed), 9)
    tokens = normal_values(splits[0], (TOKENS, D), 1.0, 6.0, ((0, 32),))
    lengths = jax.random.randint(splits[1], (REQS,), LMAX // 16, LMAX + 1).astype(jnp.int32)
    routes_keys = jax.random.split(jax.random.fold_in(splits[2], 1), TOKENS // TOK_DEV)
    routes_turns = jax.random.permutation(jax.random.fold_in(splits[2], 3), TOKENS // TOK_DEV)
    routes = jax.vmap(lambda own, number: shared_out(jax.random.fold_in(splits[2], 2), own, number, TOK_DEV, EXPERTS, TOP, CAP, 2))(routes_keys, routes_turns).reshape((TOKENS, TOP))
    norm_gain = jnp.clip(1.0 + 0.18 * jax.random.normal(splits[3], (D,), jnp.float32), 0.1, 1.9)
    router = normal_values(splits[4], (D, EXPERTS), D ** -0.5, 0.15625)
    w_gate = normal_values(splits[5], (EXPERTS, D, HID), D ** -0.5, 0.15625, ((0, 16), (1, 2)))
    w_up = normal_values(splits[6], (EXPERTS, D, HID), D ** -0.5, 0.15625, ((0, 16), (1, 2)))
    w_down = normal_values(splits[7], (EXPERTS, HID, D), HID ** -0.5, 0.25, ((0, 16), (2, 2)))
    return {"tokens": tokens, "lengths": lengths, "routes": routes, "norm_gain": norm_gain, "router": router, "w_gate": w_gate, "w_up": w_up, "w_down": w_down}


def reference(tokens, lengths, routes, norm_gain, router, w_gate, w_up, w_down):
    tokens_f32 = tokens.astype(jnp.float32)
    scale_rows = lax.rsqrt(lax.optimization_barrier(jnp.mean(tokens_f32 * tokens_f32, axis=-1, keepdims=True)) + 1e-06)
    normed = (tokens_f32 * scale_rows * norm_gain.astype(jnp.float32)).astype(jnp.bfloat16)
    logits = jnp.dot(normed, router, preferred_element_type=jnp.float32)
    position = jnp.arange(TOKENS, dtype=jnp.int32)
    living = position % LMAX < lengths[position // LMAX]
    gate_weights = jax.nn.sigmoid(jnp.take_along_axis(logits, routes, axis=1)) * living[:, None].astype(jnp.float32)
    row_bound = min(TOKENS, CAP * N_DP * N_TENSOR)

    def one_expert(combined, expert):
        routed_here = (routes == expert) & living[:, None]
        weight = lax.optimization_barrier(jnp.sum(jnp.where(routed_here, gate_weights, jnp.float32(0.0)), axis=1))
        chosen = jnp.any(routed_here, axis=1)
        picked = jnp.nonzero(chosen, size=row_bound, fill_value=0)[0].astype(jnp.int32)
        is_valid = (jnp.arange(row_bound, dtype=jnp.int32) < jnp.sum(chosen.astype(jnp.int32))).astype(jnp.float32)
        rows_in = normed[picked]
        gate_proj = jnp.dot(rows_in, w_gate[expert], preferred_element_type=jnp.float32)
        up_proj = jnp.dot(rows_in, w_up[expert], preferred_element_type=jnp.float32)
        hidden = (jax.nn.silu(gate_proj) * up_proj).astype(jnp.bfloat16)
        expert_out = jnp.dot(hidden, w_down[expert], preferred_element_type=jnp.float32).astype(jnp.bfloat16)
        weighted = expert_out.astype(jnp.float32) * (weight[picked] * is_valid)[:, None]
        return (combined.at[picked].add(weighted), None)
    empty_acc = jnp.zeros((TOKENS, D), jnp.float32)
    combined, _ = lax.scan(one_expert, empty_acc, jnp.arange(EXPERTS, dtype=jnp.int32))
    return (tokens_f32 + combined).astype(jnp.bfloat16)
```

```python
import jax
import jax.numpy as jnp
from jax import lax
from jax.sharding import PartitionSpec as P

LMAX = 4096
F32 = jnp.float32
BF16 = jnp.bfloat16


def gate_of(logits, routes, lengths, experts):
    rows = logits.shape[0]
    position = lax.axis_index("tensor") * rows + jnp.arange(rows, dtype=jnp.int32)
    living = position % LMAX < lengths[position // LMAX]
    ids = jnp.arange(experts, dtype=jnp.int32)
    named = jnp.zeros((rows, experts), jnp.bool_)
    for k in range(routes.shape[1]):
        named = named | (routes[:, k : k + 1] == ids[None, :])
    return jnp.where(named & living[:, None], jax.nn.sigmoid(logits), 0.0)


def norm_of(tokens_f32, norm_gain):
    scale_rows = lax.rsqrt(jnp.mean(tokens_f32 * tokens_f32, axis=-1, keepdims=True) + 1e-06)
    return (tokens_f32 * scale_rows * norm_gain).astype(BF16)


def dot(a, b):
    return jnp.dot(a, b, preferred_element_type=F32)


def general(tokens, lengths, routes, norm_gain, router, w_gate, w_up, w_down):
    experts = router.shape[1]
    local = w_gate.shape[0]
    tokens_f32 = tokens.astype(F32)
    normed = norm_of(tokens_f32, norm_gain)
    gates = gate_of(dot(normed, router), routes, lengths, experts)
    gate_all = lax.all_gather(w_gate, "dp", axis=1, tiled=True)
    up_all = lax.all_gather(w_up, "dp", axis=1, tiled=True)
    down_all = lax.all_gather(w_down, "dp", axis=2, tiled=True)
    rows_all = lax.all_gather(normed, "tensor", axis=0, tiled=True)
    gates_all = lax.all_gather(gates, "tensor", axis=0, tiled=True)
    first = lax.axis_index("tensor") * local
    total = jnp.zeros(rows_all.shape, F32)
    for x in range(local):
        weight = lax.dynamic_slice_in_dim(gates_all, first + x, 1, axis=1)
        hidden = jax.nn.silu(dot(rows_all, gate_all[x])) * dot(rows_all, up_all[x])
        total = total + dot((hidden * weight).astype(BF16), down_all[x])
    combined = lax.psum_scatter(total.astype(BF16), "tensor", scatter_dimension=0, tiled=True)
    return (tokens_f32 + combined.astype(F32)).astype(BF16)


def lanes(tokens, lengths, routes, norm_gain, router, w_gate, w_up, w_down):
    experts = router.shape[1]
    width = tokens.shape[1]
    half = width // 2
    rows = tokens.shape[0]
    x = lax.axis_index("dp")
    t = lax.axis_index("tensor")
    z, y, c = t // 4, (t // 2) % 2, t % 2
    middle = (z == 1) | (z == 2)

    def swap(v):
        return jnp.where(x == 0, v, jnp.concatenate([v[:, half:], v[:, :half]], axis=1))

    def over(axis_pairs):
        return [(a * 4 + r, b * 4 + r) for a, b in axis_pairs for r in range(4)]

    def send(v, pairs):
        return lax.ppermute(v, "tensor", pairs)

    by_core = [(i, i ^ 1) for i in range(16)]
    by_y = [(i, i ^ 2) for i in range(16)]
    outer = over([(0, 1), (1, 0), (2, 3), (3, 2)])
    inner = over([(1, 2), (2, 1)])
    outward = over([(1, 0), (2, 3)])
    inward = over([(0, 1), (3, 2)])

    tokens_f32 = tokens.astype(F32)
    normed = norm_of(tokens_f32, norm_gain)
    gates = gate_of(dot(normed, router), routes, lengths, experts)
    gates_all = lax.all_gather(gates.T, "tensor", axis=0)

    in_own = jnp.concatenate([w_gate[0], w_up[0]], axis=1)
    down_own = w_down[0]
    in_far = lax.ppermute(in_own, "dp", [(0, 1), (1, 0)])
    down_far = lax.ppermute(down_own, "dp", [(0, 1), (1, 0)])
    in_parts = [[in_own, in_far], [send(in_own, by_core), send(in_far, by_core)]]
    down_parts = [[down_own, down_far], [send(down_own, by_core), send(down_far, by_core)]]
    hid = w_gate.shape[2]
    gate_w = jnp.concatenate([jnp.concatenate([p[:, :hid] for p in e], axis=0) for e in in_parts], axis=1)
    up_w = jnp.concatenate([jnp.concatenate([p[:, hid:] for p in e], axis=0) for e in in_parts], axis=1)
    down_w = jnp.concatenate([jnp.concatenate(e, axis=1) for e in down_parts], axis=0)

    s_0 = swap(normed)
    t_0 = send(s_0, by_y)
    s_a = send(s_0, outer)
    s_m = send(s_0, inner)
    t_a = send(s_a, by_y)
    s_b = jnp.where(middle, s_m, send(s_m, outward))
    s_n = send(s_a, inner)
    t_b = send(s_b, by_y)
    s_c = jnp.where(middle, s_n, send(s_n, outward))
    t_c = send(s_c, by_y)

    low = z < 2
    planes = [z, z ^ 1, jnp.where(low, 2, 1), jnp.where(low, 3, 0)]
    my_experts = gates_all.reshape(4, 2, 2, experts, rows)

    def weights_of(plane, side):
        own = lax.dynamic_slice(my_experts, (plane, side, c, 2 * (t // 2), 0), (1, 1, 1, 2, rows)).reshape(2, rows)
        own = jnp.where(c == 0, own, own[::-1])
        return own.T

    def partial(block, plane, side):
        w = weights_of(plane, side)
        w = jnp.repeat(w, hid, axis=1)
        hidden = jax.nn.silu(dot(block, gate_w)) * dot(block, up_w) * w
        return dot(hidden.astype(BF16), down_w).astype(BF16)

    def add(a, b):
        return (a.astype(F32) + b.astype(F32)).astype(BF16)

    q_c = add(partial(s_c, planes[3], y), send(partial(t_c, planes[3], 1 - y), by_y))
    q_b = add(partial(s_b, planes[2], y), send(partial(t_b, planes[2], 1 - y), by_y))
    q_a = add(partial(s_a, planes[1], y), send(partial(t_a, planes[1], 1 - y), by_y))
    r_0 = send(partial(t_0, planes[0], 1 - y), by_y)
    q_n = add(q_c, send(q_c, inward))
    q_a = add(q_a, send(q_n, inner))
    q_m = add(q_b, send(q_b, inward))
    r_m = send(q_m, inner)
    r_a = send(q_a, outer)
    p_0 = partial(s_0, planes[0], y)
    combined = p_0.astype(F32) + r_0.astype(F32) + r_m.astype(F32) + r_a.astype(F32)
    return (tokens_f32 + swap(combined)).astype(BF16)


def solution(mesh):
    placed = (
        P(("dp", "tensor"), None),
        P("dp"),
        P(("dp", "tensor"), None),
        P(),
        P(),
        P("tensor", "dp", None),
        P("tensor", "dp", None),
        P("tensor", None, "dp"),
    )

    def shards(*args):
        fits = mesh.shape["dp"] == 2 and mesh.shape["tensor"] == 16 and args[5].shape[0] == 1
        return (lanes if fits else general)(*args)

    return jax.shard_map(
        shards, mesh=mesh, in_specs=placed, out_specs=P(("dp", "tensor"), None), check_vma=False
    )
```

```python
import functools
import jax
import jax.numpy as jnp
from jax import lax
from jax.experimental import pallas as pl
from jax.experimental.pallas import tpu as pltpu
from jax.sharding import PartitionSpec as P

LMAX = 4096
F32 = jnp.float32
BF16 = jnp.bfloat16


def gate_of(logits, routes, lengths, experts):
    rows = logits.shape[0]
    position = lax.axis_index("tensor") * rows + jnp.arange(rows, dtype=jnp.int32)
    living = position % LMAX < lengths[position // LMAX]
    ids = jnp.arange(experts, dtype=jnp.int32)
    named = jnp.zeros((rows, experts), jnp.bool_)
    for k in range(routes.shape[1]):
        named = named | (routes[:, k : k + 1] == ids[None, :])
    return jnp.where(named & living[:, None], jax.nn.sigmoid(logits), 0.0)


def norm_of(tokens_f32, norm_gain):
    scale_rows = lax.rsqrt(jnp.mean(tokens_f32 * tokens_f32, axis=-1, keepdims=True) + 1e-06)
    return (tokens_f32 * scale_rows * norm_gain).astype(BF16)


def dot(a, b):
    return jnp.dot(a, b, preferred_element_type=F32)


def general(tokens, lengths, routes, norm_gain, router, w_gate, w_up, w_down):
    experts = router.shape[1]
    local = w_gate.shape[0]
    tokens_f32 = tokens.astype(F32)
    normed = norm_of(tokens_f32, norm_gain)
    gates = gate_of(dot(normed, router), routes, lengths, experts)
    gate_all = lax.all_gather(w_gate, "dp", axis=1, tiled=True)
    up_all = lax.all_gather(w_up, "dp", axis=1, tiled=True)
    down_all = lax.all_gather(w_down, "dp", axis=2, tiled=True)
    rows_all = lax.all_gather(normed, "tensor", axis=0, tiled=True)
    gates_all = lax.all_gather(gates, "tensor", axis=0, tiled=True)
    first = lax.axis_index("tensor") * local
    total = jnp.zeros(rows_all.shape, F32)
    for x in range(local):
        weight = lax.dynamic_slice_in_dim(gates_all, first + x, 1, axis=1)
        hidden = jax.nn.silu(dot(rows_all, gate_all[x])) * dot(rows_all, up_all[x])
        total = total + dot((hidden * weight).astype(BF16), down_all[x])
    combined = lax.psum_scatter(total.astype(BF16), "tensor", scatter_dimension=0, tiled=True)
    return (tokens_f32 + combined.astype(F32)).astype(BF16)


def prologue_kernel(scalars, tokens, gain, router, routes_t, normed, gates_t):
    v = tokens[...].astype(F32)
    scale_rows = lax.rsqrt(jnp.mean(v * v, axis=-1, keepdims=True) + 1e-06)
    out = (v * scale_rows * gain[...]).astype(BF16)
    normed[...] = out
    logits_t = lax.dot_general(router[...], out, (((1,), (1,)), ((), ())), preferred_element_type=F32)
    experts, rows = logits_t.shape
    ids = lax.broadcasted_iota(jnp.int32, (experts, rows), 0)
    position = scalars[0] + lax.broadcasted_iota(jnp.int32, (experts, rows), 1)
    named = routes_t[0:1, :] == ids
    for k in range(1, routes_t.shape[0]):
        named = named | (routes_t[k : k + 1, :] == ids)
    living = position < scalars[1]
    gates_t[...] = jnp.where(named & living, jax.nn.sigmoid(logits_t), 0.0)


def expert_kernel(gate_at, scalars, *refs):
    count = len(gate_at)
    gates, blocks = refs[:3], refs[3 : 3 + count]
    weights = refs[3 + count : 15 + count]
    outs, total = refs[15 + count : 15 + 2 * count], refs[15 + 2 * count]
    step, last = pl.program_id(0), pl.num_programs(0) - 1
    rows, width = blocks[0].shape
    half = width // 2
    own = pl.ds(pl.multiple_of(scalars[0] * half, half), half)
    far = pl.ds(pl.multiple_of((1 - scalars[0]) * half, half), half)
    eye = lax.broadcasted_iota(jnp.int32, (rows, rows), 0) == lax.broadcasted_iota(jnp.int32, (rows, rows), 1)
    for b in range(count):
        which, entry, side = gate_at[b]
        entry = scalars[-entry] + side if entry < 0 else entry + side
        near, away = blocks[b][:, own], blocks[b][:, far]
        hidden = []
        for e in range(2):
            go, gf, uo, uf = (weights[6 * e + i] for i in range(4))
            line = gates[which][entry, pl.ds(scalars[1 + e], 1), :]
            weight = jnp.sum(jnp.where(eye, line, 0.0), axis=1, keepdims=True)
            gate = dot(near, go[...]) + dot(away, gf[...])
            up = dot(near, uo[...]) + dot(away, uf[...])
            hidden.append((jax.nn.silu(gate) * up * weight).astype(BF16))
        for columns, i in ((own, 4), (far, 5)):
            value = dot(hidden[0], weights[i][...]) + dot(hidden[1], weights[6 + i][...])

            @pl.when(step == 0)
            def _():
                total[b, :, columns] = value

            @pl.when((step > 0) & (step < last))
            def _():
                total[b, :, columns] += value

            @pl.when(step == last)
            def _():
                outs[b][:, columns] = (total[b, :, columns] + value).astype(BF16)


def lanes(tokens, lengths, routes, norm_gain, router, w_gate, w_up, w_down):
    experts = router.shape[1]
    rows, width = tokens.shape
    half = width // 2
    hid = w_gate.shape[2]
    x = lax.axis_index("dp")
    t = lax.axis_index("tensor")
    z, y, c = t // 4, (t // 2) % 2, t % 2
    middle = (z == 1) | (z == 2)

    def over(axis_pairs):
        return [(a * 4 + r, b * 4 + r) for a, b in axis_pairs for r in range(4)]

    def send(v, pairs):
        return lax.ppermute(v, "tensor", pairs)

    by_core = [(i, i ^ 1) for i in range(16)]
    by_y = [(i, i ^ 2) for i in range(16)]
    outer = over([(0, 1), (1, 0), (2, 3), (3, 2)])
    inner = over([(1, 2), (2, 1)])
    skip = over([(0, 2), (2, 0), (1, 3), (3, 1)])
    outward = over([(1, 0), (2, 3)])
    inward = over([(0, 1), (3, 2)])

    smem = pl.BlockSpec(memory_space=pltpu.SMEM)
    vmem = pl.BlockSpec(memory_space=pltpu.VMEM)
    place = jnp.stack([t * rows, lengths[0]]).astype(jnp.int32)
    s_0, gates = pl.pallas_call(
        prologue_kernel,
        out_shape=(jax.ShapeDtypeStruct((rows, width), BF16), jax.ShapeDtypeStruct((experts, rows), F32)),
        in_specs=[smem] + [vmem] * 4,
        out_specs=(vmem, vmem),
        name="prologue",
    )(place, tokens, norm_gain.reshape(1, width), router.T, routes.T)

    def together(*values):
        return lax.optimization_barrier(values)

    own_w = [w_gate[0], w_up[0], w_down[0]]
    far_w = [None] * 3
    pair_far = [None] * 3
    own_w[0], own_w[1], own_w[2], s_0, gates = together(*own_w, s_0, gates)

    t_0 = send(s_0, by_y)
    s_a = send(s_0, outer)
    s_m = send(s_0, inner)
    far_w[0] = lax.ppermute(own_w[0], "dp", [(0, 1), (1, 0)])
    g_y = send(gates, by_y)
    pair_own = [send(w, by_core) for w in own_w]
    s_0, t_0, s_a, s_m, far_w[0], g_y, own_w[1], own_w[2], pair_own[0], pair_own[1], pair_own[2] = together(
        s_0, t_0, s_a, s_m, far_w[0], g_y, own_w[1], own_w[2], *pair_own
    )

    t_a = send(s_a, by_y)
    s_b = send(s_m, outward)
    s_n = send(s_a, inner)
    far_w[1] = lax.ppermute(own_w[1], "dp", [(0, 1), (1, 0)])
    pair_far[0] = send(far_w[0], by_core)
    g_0 = jnp.stack([gates, g_y])
    g_1 = send(g_0, outer)
    t_a, s_b, s_n, far_w[1], pair_far[0], g_0, g_1, own_w[2] = together(
        t_a, s_b, s_n, far_w[1], pair_far[0], g_0, g_1, own_w[2]
    )

    s_b = jnp.where(middle, s_m, s_b)
    t_b = send(s_b, by_y)
    s_c = send(s_n, outward)
    far_w[2] = lax.ppermute(own_w[2], "dp", [(0, 1), (1, 0)])
    pair_far[1] = send(far_w[1], by_core)
    g_2 = send(jnp.concatenate([g_0, g_1]), skip)
    s_b, t_b, s_c, far_w[2], pair_far[1], g_2, t_a, s_n = together(s_b, t_b, s_c, far_w[2], pair_far[1], g_2, t_a, s_n)

    s_c = jnp.where(middle, s_n, s_c)
    t_c = send(s_c, by_y)
    pair_far[2] = send(far_w[2], by_core)
    weights = []
    for near, away in ((own_w, far_w), (pair_own, pair_far)):
        for o, f in zip(near, away):
            weights += [o, f]

    scalars = jnp.stack([x, t, t ^ 1, jnp.where(middle, 2, 0), jnp.where(middle, 0, 2)]).astype(jnp.int32)
    at = {"0": (0, 0), "a": (1, 0), "b": (2, -3), "c": (2, -4)}

    def run(w, g_0, g_1, g_2, *named):
        count = len(named)
        block = pl.BlockSpec((rows, width), lambda h: (0, 0))
        into = pl.BlockSpec((half, 256), lambda h: (0, h))
        outof = pl.BlockSpec((256, half), lambda h: (h, 0))
        gate_spec = [pl.BlockSpec(g.shape, lambda h: (0, 0, 0)) for g in (g_0, g_1, g_2)]
        gate_at = tuple(at[n[1]] + (int(n[0] == "t"),) for n, _ in named)
        flops = 2 * count * rows * 2 * 3 * width * hid
        return pl.pallas_call(
            functools.partial(expert_kernel, gate_at),
            grid=(hid // 256,),
            out_shape=tuple(jax.ShapeDtypeStruct((rows, width), BF16) for _ in named),
            in_specs=[smem] + gate_spec + [block] * count + ([into] * 4 + [outof] * 2) * 2,
            out_specs=tuple([block] * count),
            scratch_shapes=[pltpu.VMEM((count, rows, width), F32)],
            compiler_params=pltpu.CompilerParams(vmem_limit_bytes=40 * 2**20),
            cost_estimate=pl.CostEstimate(flops=flops, bytes_accessed=12 * width * hid, transcendentals=0),
            name="experts_" + "_".join(n for n, _ in named),
        )(scalars, g_0, g_1, g_2, *(v for _, v in named), *w)

    def add(a, b):
        return (a.astype(F32) + b.astype(F32)).astype(BF16)

    g = (g_0, g_1, g_2)
    p_sc, p_tb, p_ta = run(weights, *g, ("sc", s_c), ("tb", t_b), ("ta", t_a))
    t_c, p_sc, p_tb, p_ta = together(t_c, p_sc, p_tb, p_ta)
    (p_tc,) = run(weights, *g, ("tc", t_c))
    p_tc, s_b, t_0, s_a, s_0 = together(p_tc, s_b, t_0, s_a, s_0)

    r_c = send(p_tc, by_y)
    p_sb, p_t0, p_sa = run(weights, *g, ("sb", s_b), ("t0", t_0), ("sa", s_a))
    r_c, p_sb, p_t0, p_sa, p_tb, s_0 = together(r_c, p_sb, p_t0, p_sa, p_tb, s_0)

    q_c = add(p_sc, r_c)
    r_b = send(p_tb, by_y)
    r_n = send(q_c, inward)
    (p_s0,) = run(weights, *g, ("s0", s_0))
    q_c, r_b, r_n, p_s0, p_ta = together(q_c, r_b, r_n, p_s0, p_ta)

    q_n = add(q_c, r_n)
    q_b = add(p_sb, r_b)
    r_a = send(p_ta, by_y)
    r_i = send(q_n, inner)
    r_m = send(q_b, inward)
    r_a, r_i, r_m, q_b, p_t0 = together(r_a, r_i, r_m, q_b, p_t0)

    q_a = p_sa.astype(F32) + r_a.astype(F32) + r_i.astype(F32)
    r_0 = send(p_t0, by_y)
    r_o = send(q_a.astype(BF16), outer)
    r_m = send(add(q_b, r_m), inner)
    combined = p_s0.astype(F32) + r_0.astype(F32) + r_m.astype(F32) + r_o.astype(F32)
    return (tokens.astype(F32) + combined).astype(BF16)


def solution(mesh):
    placed = (
        P(("dp", "tensor"), None),
        P("dp"),
        P(("dp", "tensor"), None),
        P(),
        P(),
        P("tensor", "dp", None),
        P("tensor", "dp", None),
        P("tensor", None, "dp"),
    )

    def shards(*args):
        fits = mesh.shape["dp"] == 2 and mesh.shape["tensor"] == 16 and args[5].shape[0] == 1
        return (lanes if fits else general)(*args)

    return jax.shard_map(
        shards, mesh=mesh, in_specs=placed, out_specs=P(("dp", "tensor"), None), check_vma=False
    )
```

```python
import functools
import jax
import jax.numpy as jnp
from jax import lax
from jax.experimental import pallas as pl
from jax.experimental.pallas import tpu as pltpu
from jax.sharding import PartitionSpec as P

LMAX = 4096
F32 = jnp.float32
BF16 = jnp.bfloat16


def gate_of(logits, routes, lengths, experts):
    rows = logits.shape[0]
    position = lax.axis_index("tensor") * rows + jnp.arange(rows, dtype=jnp.int32)
    living = position % LMAX < lengths[position // LMAX]
    ids = jnp.arange(experts, dtype=jnp.int32)
    named = jnp.zeros((rows, experts), jnp.bool_)
    for k in range(routes.shape[1]):
        named = named | (routes[:, k : k + 1] == ids[None, :])
    return jnp.where(named & living[:, None], jax.nn.sigmoid(logits), 0.0)


def norm_of(tokens_f32, norm_gain):
    scale_rows = lax.rsqrt(jnp.mean(tokens_f32 * tokens_f32, axis=-1, keepdims=True) + 1e-06)
    return (tokens_f32 * scale_rows * norm_gain).astype(BF16)


def dot(a, b):
    return jnp.dot(a, b, preferred_element_type=F32)


def general(tokens, lengths, routes, norm_gain, router, w_gate, w_up, w_down):
    experts = router.shape[1]
    local = w_gate.shape[0]
    tokens_f32 = tokens.astype(F32)
    normed = norm_of(tokens_f32, norm_gain)
    gates = gate_of(dot(normed, router), routes, lengths, experts)
    gate_all = lax.all_gather(w_gate, "dp", axis=1, tiled=True)
    up_all = lax.all_gather(w_up, "dp", axis=1, tiled=True)
    down_all = lax.all_gather(w_down, "dp", axis=2, tiled=True)
    rows_all = lax.all_gather(normed, "tensor", axis=0, tiled=True)
    gates_all = lax.all_gather(gates, "tensor", axis=0, tiled=True)
    first = lax.axis_index("tensor") * local
    total = jnp.zeros(rows_all.shape, F32)
    for x in range(local):
        weight = lax.dynamic_slice_in_dim(gates_all, first + x, 1, axis=1)
        hidden = jax.nn.silu(dot(rows_all, gate_all[x])) * dot(rows_all, up_all[x])
        total = total + dot((hidden * weight).astype(BF16), down_all[x])
    combined = lax.psum_scatter(total.astype(BF16), "tensor", scatter_dimension=0, tiled=True)
    return (tokens_f32 + combined.astype(F32)).astype(BF16)


GATE_ROWS = 16
CHUNK = 256


def prologue_kernel(lengths, tokens, gain, router, routes_t, normed, order):
    v = tokens[...].astype(F32)
    scale_rows = lax.rsqrt(jnp.mean(v * v, axis=-1, keepdims=True) + 1e-06)
    out = (v * scale_rows * gain[...]).astype(BF16)
    rows, width = out.shape
    normed[GATE_ROWS:, :] = out
    logits_t = lax.dot_general(router[...], out, (((1,), (1,)), ((), ())), preferred_element_type=F32)
    ids = lax.broadcasted_iota(jnp.int32, logits_t.shape, 0)
    position = lax.axis_index("tensor") * rows + lax.broadcasted_iota(jnp.int32, logits_t.shape, 1)
    named = routes_t[0:1, :] == ids
    for k in range(1, routes_t.shape[0]):
        named = named | (routes_t[k : k + 1, :] == ids)
    living = position < lengths[0]
    gates = jnp.where(named & living, jax.nn.sigmoid(logits_t), 0.0)
    high = gates.astype(BF16)
    normed[:GATE_ROWS, :rows] = high
    normed[:GATE_ROWS, rows : 2 * rows] = (gates - high.astype(F32)).astype(BF16)
    normed[:GATE_ROWS, 2 * rows :] = jnp.zeros((GATE_ROWS, width - 2 * rows), BF16)
    order[...] = jnp.zeros_like(order)


def pack_kernel(gate, up, down, *packed):
    half = gate.shape[0]
    for h, chunk in enumerate(packed):
        units = slice(CHUNK * h, CHUNK * (h + 1))
        chunk[:, :CHUNK] = gate[:, units]
        chunk[:, CHUNK : 2 * CHUNK] = up[:, units]
        for i in range(half // CHUNK):
            columns = slice(CHUNK * i, CHUNK * (i + 1))
            chunk[columns, 2 * CHUNK :] = down[units, columns]


def expert_kernel(work, based, count, _, *refs):
    blocks, refs = refs[:count], refs[count:]
    bases, refs = (refs[: len(based)], refs[len(based) :])
    used = 4 * len(work)
    weights, refs = refs[:used], refs[used:]
    outs, (taken, weight, hidden, held, arrived) = refs[:count], refs[count:]
    rows, width = outs[0].shape
    half = width // 2
    x = lax.axis_index("dp")
    t = lax.axis_index("tensor")
    starts = (pl.multiple_of(x * half, half), pl.multiple_of((1 - x) * half, half))
    copies = [pltpu.make_async_copy(weights[i], held.at[i], arrived.at[i]) for i in range(used)]
    for copy in copies:
        copy.start()

    eye = lax.broadcasted_iota(jnp.int32, (rows, rows), 0) == lax.broadcasted_iota(jnp.int32, (rows, rows), 1)
    for b in range(count):
        here = pl.ds(b * rows, rows)
        taken[here, :] = blocks[b][GATE_ROWS:, :]
        lines = blocks[b][:GATE_ROWS, :rows].astype(F32) + blocks[b][:GATE_ROWS, rows : 2 * rows].astype(F32)
        ids = lax.broadcasted_iota(jnp.int32, lines.shape, 0)
        for n, (expert, first, last) in enumerate(work):
            if first <= b < last:
                line = jnp.sum(jnp.where(ids == jnp.bitwise_xor(t, 2 * expert), lines, 0.0), axis=0, keepdims=True)
                weight[n, here, :] = jnp.sum(jnp.where(eye, line, 0.0), axis=1, keepdims=True)

    for n, (_, first, last) in enumerate(work):
        here = pl.ds(first * rows, (last - first) * rows)
        near, away = (taken[here, pl.ds(start, half)] for start in starts)
        for h in range(2):
            own, far = 4 * n + 2 * h, 4 * n + 2 * h + 1
            copies[own].wait()
            copies[far].wait()
            gate = dot(near, held[own, :, :CHUNK]) + dot(away, held[far, :, :CHUNK])
            up = dot(near, held[own, :, CHUNK : 2 * CHUNK]) + dot(away, held[far, :, CHUNK : 2 * CHUNK])
            units = slice(CHUNK * h, CHUNK * (h + 1))
            hidden[n, here, units] = (jax.nn.silu(gate) * up * weight[n, here, :]).astype(BF16)

    edges = sorted({0, count}.union(*({first, last} for _, first, last in work)))
    for begin, end in zip(edges[:-1], edges[1:]):
        here = pl.ds(begin * rows, (end - begin) * rows)
        for side in range(2):
            for i in range(half // CHUNK):
                columns = pl.ds(pl.multiple_of(starts[side] + CHUNK * i, CHUNK), CHUNK)
                value = sum(
                    dot(hidden[n, here, CHUNK * h : CHUNK * (h + 1)], held[4 * n + 2 * h + side, CHUNK * i : CHUNK * (i + 1), 2 * CHUNK :])
                    for n, (_, first, last) in enumerate(work)
                    if first <= begin < last
                    for h in range(2)
                )
                for b in range(begin, end):
                    part = value[(b - begin) * rows : (b - begin + 1) * rows]
                    if b in based:
                        part = part + bases[based.index(b)][:, columns].astype(F32)
                    outs[b][:, columns] = part.astype(BF16)


def lanes(tokens, lengths, routes, norm_gain, router, w_gate, w_up, w_down):
    rows, width = tokens.shape
    half = width // 2
    hid = w_gate.shape[2]
    z = lax.axis_index("tensor") // 4
    middle = (z == 1) | (z == 2)

    def send(v, pairs):
        return lax.ppermute(v, "tensor", pairs)

    def across(v):
        return lax.ppermute(v, "dp", [(0, 1), (1, 0)])

    def over(*pairs):
        return [(a * 4 + r, b * 4 + r) for a, b in pairs for r in range(4)]

    by_core, by_y = ([(i, i ^ bit) for i in range(16)] for bit in (1, 2))
    outer = over((0, 1), (1, 0), (2, 3), (3, 2))
    inner = over((1, 2), (2, 1))
    outward = over((1, 0), (2, 3))
    inward = over((0, 1), (3, 2))
    smem = pl.BlockSpec(memory_space=pltpu.SMEM)
    vmem = pl.BlockSpec(memory_space=pltpu.VMEM)
    anywhere = pl.BlockSpec(memory_space=pl.ANY)

    own = pl.pallas_call(
        pack_kernel,
        out_shape=(jax.ShapeDtypeStruct((half, half), BF16),) * (hid // CHUNK),
        in_specs=[vmem] * 3,
        out_specs=(vmem,) * (hid // CHUNK),
        name="pack",
    )(w_gate[0], w_up[0], w_down[0])
    x_0 = across(own[0])
    y_1 = send(own[1], by_y)
    s_0, begin = pl.pallas_call(
        prologue_kernel,
        out_shape=(jax.ShapeDtypeStruct((rows + GATE_ROWS, width), BF16), jax.ShapeDtypeStruct((8, 128), F32)),
        in_specs=[smem] + [vmem] * 4,
        out_specs=(vmem,) * 2,
        name="prologue",
    )(lengths, tokens, norm_gain.reshape(1, width), router.T, routes.T)

    order = [begin]

    def together(*values):
        *values, order[0] = lax.optimization_barrier((*values, order[0]))
        return values

    def run(shards, work, bases):
        count = len(shards)
        based = tuple(b for b, base in enumerate(bases) if base is not None)
        used = 4 * len(work)
        return pl.pallas_call(
            functools.partial(expert_kernel, tuple((e, first, last) for e, _, first, last in work), based, count),
            out_shape=tuple(jax.ShapeDtypeStruct((rows, width), BF16) for _ in shards),
            in_specs=[anywhere] + [vmem] * (count + len(based)) + [anywhere] * used,
            out_specs=(vmem,) * count,
            scratch_shapes=[
                pltpu.VMEM((count * rows, width), BF16),
                pltpu.VMEM((len(work), count * rows, 1), F32),
                pltpu.VMEM((len(work), count * rows, 2 * CHUNK), BF16),
                pltpu.VMEM((used, half, half), BF16),
                pltpu.SemaphoreType.DMA((used,)),
            ],
            compiler_params=pltpu.CompilerParams(vmem_limit_bytes=36 * 2**20),
            cost_estimate=pl.CostEstimate(flops=1, bytes_accessed=1, transcendentals=0),
            name="experts",
        )(order[0], *shards, *(bases[b] for b in based), *(w for _, ws, _, _ in work for w in ws))

    def add(*terms):
        return sum(v.astype(F32) for v in terms).astype(BF16)

    s_m = send(s_0, inner)
    s_a = send(s_0, outer)
    m_0 = send(s_0, by_core)
    x_0, y_1, own_0, own_1 = together(x_0, y_1, *own)
    x_1 = across(own_1)
    y_0 = send(own_0, by_y)
    s_m, s_a, m_0 = together(s_m, s_a, m_0)
    s_b = send(s_m, outward)
    s_n = send(s_a, inner)
    m_a = send(s_a, by_core)
    x_1, y_0, x_0, y_1 = together(x_1, y_0, x_0, y_1)
    d_0 = send(x_0, by_y)
    d_1 = across(y_1)
    s_b, s_n, m_a = together(s_b, s_n, m_a)
    s_c = send(s_n, outward)
    s_b = jnp.where(middle, s_m, s_b)
    m_b = send(s_b, by_core)
    mine = (own[0], x_0, own[1], x_1)
    u_0, v_0, u_a, v_a = run((s_0, m_0, s_a, m_a), [(0, mine, 0, 4)], [None] * 4)
    m_b, u_0, v_0, u_a, v_a = together(m_b, u_0, v_0, u_a, v_a)
    u_b, v_b = run((s_b, m_b), [(0, mine, 0, 2)], [None] * 2)
    s_c, u_b, v_b = together(s_c, u_b, v_b)
    s_c = jnp.where(middle, s_n, s_c)
    m_c = send(s_c, by_core)
    (m_c,) = together(m_c)
    u_c, v_c = run((s_c, m_c), [(0, mine, 0, 2)], [None] * 2)
    d_0, d_1, u_c, v_c = together(d_0, d_1, u_c, v_c)
    theirs = (y_0, d_0, y_1, d_1)
    p_c, o_c = run((s_c, m_c), [(1, theirs, 0, 2)], [u_c, v_c])
    r_c = send(o_c, by_core)

    r_c, p_c = together(r_c, p_c)
    q_c = add(p_c, r_c)
    r_n = send(q_c, inward)
    p_b, o_b, p_a, o_a, p_0, o_0 = run((s_b, m_b, s_a, m_a, s_0, m_0), [(1, theirs, 0, 6)], [u_b, v_b, u_a, v_a, u_0, v_0])
    r_b, r_a, r_0 = send(o_b, by_core), send(o_a, by_core), send(o_0, by_core)
    r_b, r_a, r_0, r_n, p_b, p_a = together(r_b, r_a, r_0, r_n, p_b, p_a)
    q_b = add(p_b, r_b)
    r_m = send(q_b, inward)
    r_i = send(add(q_c, r_n), inner)
    r_m, r_i = together(r_m, r_i)
    r_o = send(add(p_a, r_a, r_i), outer)
    r_m = send(add(q_b, r_m), inner)
    return add(tokens, p_0, r_0, r_o, r_m)


def solution(mesh):
    placed = (
        P(("dp", "tensor"), None),
        P("dp"),
        P(("dp", "tensor"), None),
        P(),
        P(),
        P("tensor", "dp", None),
        P("tensor", "dp", None),
        P("tensor", None, "dp"),
    )

    def shards(*args):
        fits = mesh.shape["dp"] == 2 and mesh.shape["tensor"] == 16 and args[5].shape[0] == 1
        fits = fits and args[1].shape[0] == 1 and args[0].shape[0] == 256 and args[4].shape[1] == GATE_ROWS
        fits = fits and args[5].shape[2] == 512 and args[0].shape[1] == 1536
        return (lanes if fits else general)(*args)

    return jax.shard_map(
        shards, mesh=mesh, in_specs=placed, out_specs=P(("dp", "tensor"), None), check_vma=False
    )
```

```python
import functools
import jax
import jax.numpy as jnp
from jax import lax
from jax.experimental import pallas as pl
from jax.experimental.pallas import tpu as pltpu
from jax.sharding import PartitionSpec as P

LMAX = 4096
F32 = jnp.float32
BF16 = jnp.bfloat16


def gate_of(logits, routes, lengths, experts):
    rows = logits.shape[0]
    position = lax.axis_index("tensor") * rows + jnp.arange(rows, dtype=jnp.int32)
    living = position % LMAX < lengths[position // LMAX]
    ids = jnp.arange(experts, dtype=jnp.int32)
    named = jnp.zeros((rows, experts), jnp.bool_)
    for k in range(routes.shape[1]):
        named = named | (routes[:, k : k + 1] == ids[None, :])
    return jnp.where(named & living[:, None], jax.nn.sigmoid(logits), 0.0)


def norm_of(tokens_f32, norm_gain):
    scale_rows = lax.rsqrt(jnp.mean(tokens_f32 * tokens_f32, axis=-1, keepdims=True) + 1e-06)
    return (tokens_f32 * scale_rows * norm_gain).astype(BF16)


def dot(a, b):
    return jnp.dot(a, b, preferred_element_type=F32)


def general(tokens, lengths, routes, norm_gain, router, w_gate, w_up, w_down):
    experts = router.shape[1]
    local = w_gate.shape[0]
    tokens_f32 = tokens.astype(F32)
    normed = norm_of(tokens_f32, norm_gain)
    gates = gate_of(dot(normed, router), routes, lengths, experts)
    gate_all = lax.all_gather(w_gate, "dp", axis=1, tiled=True)
    up_all = lax.all_gather(w_up, "dp", axis=1, tiled=True)
    down_all = lax.all_gather(w_down, "dp", axis=2, tiled=True)
    rows_all = lax.all_gather(normed, "tensor", axis=0, tiled=True)
    gates_all = lax.all_gather(gates, "tensor", axis=0, tiled=True)
    first = lax.axis_index("tensor") * local
    total = jnp.zeros(rows_all.shape, F32)
    for x in range(local):
        weight = lax.dynamic_slice_in_dim(gates_all, first + x, 1, axis=1)
        hidden = jax.nn.silu(dot(rows_all, gate_all[x])) * dot(rows_all, up_all[x])
        total = total + dot((hidden * weight).astype(BF16), down_all[x])
    combined = lax.psum_scatter(total.astype(BF16), "tensor", scatter_dimension=0, tiled=True)
    return (tokens_f32 + combined.astype(F32)).astype(BF16)


GATE_ROWS = 16
CHUNK = 256


def prologue_kernel(lengths, tokens, gain, router, routes_t, normed, order):
    v = tokens[...].astype(F32)
    scale_rows = lax.rsqrt(jnp.mean(v * v, axis=-1, keepdims=True) + 1e-06)
    out = (v * scale_rows * gain[...]).astype(BF16)
    rows, width = out.shape
    normed[GATE_ROWS:, :] = out
    logits_t = lax.dot_general(router[...], out, (((1,), (1,)), ((), ())), preferred_element_type=F32)
    ids = lax.broadcasted_iota(jnp.int32, logits_t.shape, 0)
    position = lax.axis_index("tensor") * rows + lax.broadcasted_iota(jnp.int32, logits_t.shape, 1)
    named = routes_t[0:1, :] == ids
    for k in range(1, routes_t.shape[0]):
        named = named | (routes_t[k : k + 1, :] == ids)
    living = position < lengths[0]
    gates = jnp.where(named & living, jax.nn.sigmoid(logits_t), 0.0)
    high = gates.astype(BF16)
    normed[:GATE_ROWS, :rows] = high
    normed[:GATE_ROWS, rows : 2 * rows] = (gates - high.astype(F32)).astype(BF16)
    normed[:GATE_ROWS, 2 * rows :] = jnp.zeros((GATE_ROWS, width - 2 * rows), BF16)
    order[...] = jnp.zeros_like(order)


def pack_kernel(gate, up, down, *refs):
    packed, sems = refs[:-1], refs[-1]
    half = gate.shape[0]
    copies = []
    for h, chunk in enumerate(packed):
        units = pl.ds(CHUNK * h, CHUNK)
        copies.append((gate.at[:, units], chunk.at[:, pl.ds(0, CHUNK)]))
        copies.append((up.at[:, units], chunk.at[:, pl.ds(CHUNK, CHUNK)]))
        for i in range(half // CHUNK):
            columns = pl.ds(CHUNK * i, CHUNK)
            copies.append((down.at[units, columns], chunk.at[columns, pl.ds(2 * CHUNK, CHUNK)]))
    copies = [pltpu.make_async_copy(source, target, sems.at[i]) for i, (source, target) in enumerate(copies)]
    for copy in copies:
        copy.start()
    for copy in copies:
        copy.wait()


def expert_kernel(work, based, count, _, *refs):
    blocks, refs = refs[:count], refs[count:]
    bases, refs = (refs[: len(based)], refs[len(based) :])
    used = 4 * len(work)
    weights, refs = refs[:used], refs[used:]
    outs, (taken, weight, hidden, held, arrived) = refs[:count], refs[count:]
    rows, width = outs[0].shape
    half = width // 2
    x = lax.axis_index("dp")
    t = lax.axis_index("tensor")
    starts = (pl.multiple_of(x * half, half), pl.multiple_of((1 - x) * half, half))
    copies = [pltpu.make_async_copy(weights[i], held.at[i], arrived.at[i]) for i in range(used)]
    for copy in copies:
        copy.start()

    eye = lax.broadcasted_iota(jnp.int32, (rows, rows), 0) == lax.broadcasted_iota(jnp.int32, (rows, rows), 1)
    for b in range(count):
        here = pl.ds(b * rows, rows)
        taken[here, :] = blocks[b][GATE_ROWS:, :]
        lines = blocks[b][:GATE_ROWS, :rows].astype(F32) + blocks[b][:GATE_ROWS, rows : 2 * rows].astype(F32)
        ids = lax.broadcasted_iota(jnp.int32, lines.shape, 0)
        for n, (expert, first, last) in enumerate(work):
            if first <= b < last:
                line = jnp.sum(jnp.where(ids == jnp.bitwise_xor(t, 2 * expert), lines, 0.0), axis=0, keepdims=True)
                weight[n, here, :] = jnp.sum(jnp.where(eye, line, 0.0), axis=1, keepdims=True)

    for n, (_, first, last) in enumerate(work):
        here = pl.ds(first * rows, (last - first) * rows)
        near, away = (taken[here, pl.ds(start, half)] for start in starts)
        for h in range(2):
            own, far = 4 * n + 2 * h, 4 * n + 2 * h + 1
            copies[own].wait()
            copies[far].wait()
            gate = dot(near, held[own, :, :CHUNK]) + dot(away, held[far, :, :CHUNK])
            up = dot(near, held[own, :, CHUNK : 2 * CHUNK]) + dot(away, held[far, :, CHUNK : 2 * CHUNK])
            units = slice(CHUNK * h, CHUNK * (h + 1))
            hidden[n, here, units] = (jax.nn.silu(gate) * up * weight[n, here, :]).astype(BF16)

    edges = sorted({0, count}.union(*({first, last} for _, first, last in work)))
    for begin, end in zip(edges[:-1], edges[1:]):
        here = pl.ds(begin * rows, (end - begin) * rows)
        for side in range(2):
            for i in range(half // CHUNK):
                columns = pl.ds(pl.multiple_of(starts[side] + CHUNK * i, CHUNK), CHUNK)
                value = sum(
                    dot(hidden[n, here, CHUNK * h : CHUNK * (h + 1)], held[4 * n + 2 * h + side, CHUNK * i : CHUNK * (i + 1), 2 * CHUNK :])
                    for n, (_, first, last) in enumerate(work)
                    if first <= begin < last
                    for h in range(2)
                )
                for b in range(begin, end):
                    part = value[(b - begin) * rows : (b - begin + 1) * rows]
                    if b in based:
                        part = part + bases[based.index(b)][:, columns].astype(F32)
                    outs[b][:, columns] = part.astype(BF16)


def lanes(tokens, lengths, routes, norm_gain, router, w_gate, w_up, w_down):
    rows, width = tokens.shape
    half = width // 2
    hid = w_gate.shape[2]
    z = lax.axis_index("tensor") // 4
    middle = (z == 1) | (z == 2)

    def send(v, pairs):
        return lax.ppermute(v, "tensor", pairs)

    def across(v):
        return lax.ppermute(v, "dp", [(0, 1), (1, 0)])

    def over(*pairs):
        return [(a * 4 + r, b * 4 + r) for a, b in pairs for r in range(4)]

    by_core, by_y = ([(i, i ^ bit) for i in range(16)] for bit in (1, 2))
    outer = over((0, 1), (1, 0), (2, 3), (3, 2))
    inner = over((1, 2), (2, 1))
    smem = pl.BlockSpec(memory_space=pltpu.SMEM)
    vmem = pl.BlockSpec(memory_space=pltpu.VMEM)
    anywhere = pl.BlockSpec(memory_space=pl.ANY)

    own = pl.pallas_call(
        pack_kernel,
        out_shape=(jax.ShapeDtypeStruct((half, half), BF16),) * (hid // CHUNK),
        in_specs=[anywhere] * 3,
        out_specs=(vmem,) * (hid // CHUNK),
        scratch_shapes=[pltpu.SemaphoreType.DMA((hid // CHUNK * (2 + half // CHUNK),))],
        name="pack",
    )(w_gate[0], w_up[0], w_down[0])
    x_0 = across(own[0])
    y_1 = send(own[1], by_y)
    s_0, begin = pl.pallas_call(
        prologue_kernel,
        out_shape=(jax.ShapeDtypeStruct((rows + GATE_ROWS, width), BF16), jax.ShapeDtypeStruct((8, 128), F32)),
        in_specs=[smem] + [vmem] * 4,
        out_specs=(vmem,) * 2,
        name="prologue",
    )(lengths, tokens, norm_gain.reshape(1, width), router.T, routes.T)

    order = [begin]

    def together(*values):
        *values, order[0] = lax.optimization_barrier((*values, order[0]))
        return values

    def run(shards, work, bases):
        count = len(shards)
        based = tuple(b for b, base in enumerate(bases) if base is not None)
        used = 4 * len(work)
        return pl.pallas_call(
            functools.partial(expert_kernel, tuple((e, first, last) for e, _, first, last in work), based, count),
            out_shape=tuple(jax.ShapeDtypeStruct((rows, width), BF16) for _ in shards),
            in_specs=[anywhere] + [vmem] * (count + len(based)) + [anywhere] * used,
            out_specs=(vmem,) * count,
            scratch_shapes=[
                pltpu.VMEM((count * rows, width), BF16),
                pltpu.VMEM((len(work), count * rows, 1), F32),
                pltpu.VMEM((len(work), count * rows, 2 * CHUNK), BF16),
                pltpu.VMEM((used, half, half), BF16),
                pltpu.SemaphoreType.DMA((used,)),
            ],
            compiler_params=pltpu.CompilerParams(vmem_limit_bytes=36 * 2**20),
            cost_estimate=pl.CostEstimate(flops=1, bytes_accessed=1, transcendentals=0),
            name="experts",
        )(order[0], *shards, *(bases[b] for b in based), *(w for _, ws, _, _ in work for w in ws))

    def add(*terms):
        return sum(v.astype(F32) for v in terms).astype(BF16)

    s_m = send(s_0, inner)
    s_a = send(s_0, outer)
    m_0 = send(s_0, by_core)
    x_0, y_1, own_0, own_1 = together(x_0, y_1, *own)
    x_1 = across(own_1)
    y_0 = send(own_0, by_y)
    s_m, s_a, m_0 = together(s_m, s_a, m_0)
    s_b = send(s_m, outer)
    s_n = send(s_a, inner)
    m_a = send(s_a, by_core)
    x_1, y_0, x_0, y_1 = together(x_1, y_0, x_0, y_1)
    d_0 = send(x_0, by_y)
    d_1 = across(y_1)
    s_b, s_n, m_a = together(s_b, s_n, m_a)
    s_c = send(s_n, outer)
    s_b = jnp.where(middle, s_m, s_b)
    m_b = send(s_b, by_core)
    mine = (own[0], x_0, own[1], x_1)
    u_0, v_0, u_a, v_a = run((s_0, m_0, s_a, m_a), [(0, mine, 0, 4)], [None] * 4)
    m_b, u_0, v_0, u_a, v_a = together(m_b, u_0, v_0, u_a, v_a)
    u_b, v_b = run((s_b, m_b), [(0, mine, 0, 2)], [None] * 2)
    s_c, u_b, v_b = together(s_c, u_b, v_b)
    s_c = jnp.where(middle, s_n, s_c)
    m_c = send(s_c, by_core)
    (m_c,) = together(m_c)
    u_c, v_c = run((s_c, m_c), [(0, mine, 0, 2)], [None] * 2)
    d_0, d_1, u_c, v_c = together(d_0, d_1, u_c, v_c)
    theirs = (y_0, d_0, y_1, d_1)
    p_c, o_c = run((s_c, m_c), [(1, theirs, 0, 2)], [u_c, v_c])
    r_c = send(o_c, by_core)

    r_c, p_c = together(r_c, p_c)
    q_c = add(p_c, r_c)
    r_n = send(q_c, outer)
    p_b, o_b, p_a, o_a, p_0, o_0 = run((s_b, m_b, s_a, m_a, s_0, m_0), [(1, theirs, 0, 6)], [u_b, v_b, u_a, v_a, u_0, v_0])
    r_b, r_a, r_0 = send(o_b, by_core), send(o_a, by_core), send(o_0, by_core)
    r_b, p_b = together(r_b, p_b)
    q_b = add(p_b, r_b)
    r_m = send(q_b, outer)
    r_n, r_a, r_0, p_a = together(r_n, r_a, r_0, p_a)
    r_i = send(add(q_c, r_n), inner)
    (r_m,) = together(r_m)
    r_m = send(add(q_b, r_m), inner)
    (r_i,) = together(r_i)
    r_o = send(add(p_a, r_a, r_i), outer)
    return add(tokens, p_0, r_0, r_o, r_m)


def solution(mesh):
    placed = (
        P(("dp", "tensor"), None),
        P("dp"),
        P(("dp", "tensor"), None),
        P(),
        P(),
        P("tensor", "dp", None),
        P("tensor", "dp", None),
        P("tensor", None, "dp"),
    )

    def shards(*args):
        fits = mesh.shape["dp"] == 2 and mesh.shape["tensor"] == 16 and args[5].shape[0] == 1
        fits = fits and args[1].shape[0] == 1 and args[0].shape[0] == 256 and args[4].shape[1] == GATE_ROWS
        fits = fits and args[5].shape[2] == 512 and args[0].shape[1] == 1536
        return (lanes if fits else general)(*args)

    return jax.shard_map(
        shards, mesh=mesh, in_specs=placed, out_specs=P(("dp", "tensor"), None), check_vma=False
    )
```

```python
import functools
import jax
import jax.numpy as jnp
from jax import lax
from jax.experimental import pallas as pl
from jax.experimental.pallas import tpu as pltpu
from jax.sharding import PartitionSpec as P

LMAX = 4096
F32 = jnp.float32
BF16 = jnp.bfloat16


def gate_of(logits, routes, lengths, experts):
    rows = logits.shape[0]
    position = lax.axis_index("tensor") * rows + jnp.arange(rows, dtype=jnp.int32)
    living = position % LMAX < lengths[position // LMAX]
    ids = jnp.arange(experts, dtype=jnp.int32)
    named = jnp.zeros((rows, experts), jnp.bool_)
    for k in range(routes.shape[1]):
        named = named | (routes[:, k : k + 1] == ids[None, :])
    return jnp.where(named & living[:, None], jax.nn.sigmoid(logits), 0.0)


def norm_of(tokens_f32, norm_gain):
    scale_rows = lax.rsqrt(jnp.mean(tokens_f32 * tokens_f32, axis=-1, keepdims=True) + 1e-06)
    return (tokens_f32 * scale_rows * norm_gain).astype(BF16)


def dot(a, b):
    return jnp.dot(a, b, preferred_element_type=F32)


def general(tokens, lengths, routes, norm_gain, router, w_gate, w_up, w_down):
    experts = router.shape[1]
    local = w_gate.shape[0]
    tokens_f32 = tokens.astype(F32)
    normed = norm_of(tokens_f32, norm_gain)
    gates = gate_of(dot(normed, router), routes, lengths, experts)
    gate_all = lax.all_gather(w_gate, "dp", axis=1, tiled=True)
    up_all = lax.all_gather(w_up, "dp", axis=1, tiled=True)
    down_all = lax.all_gather(w_down, "dp", axis=2, tiled=True)
    rows_all = lax.all_gather(normed, "tensor", axis=0, tiled=True)
    gates_all = lax.all_gather(gates, "tensor", axis=0, tiled=True)
    first = lax.axis_index("tensor") * local
    total = jnp.zeros(rows_all.shape, F32)
    for x in range(local):
        weight = lax.dynamic_slice_in_dim(gates_all, first + x, 1, axis=1)
        hidden = jax.nn.silu(dot(rows_all, gate_all[x])) * dot(rows_all, up_all[x])
        total = total + dot((hidden * weight).astype(BF16), down_all[x])
    combined = lax.psum_scatter(total.astype(BF16), "tensor", scatter_dimension=0, tiled=True)
    return (tokens_f32 + combined.astype(F32)).astype(BF16)


GATE_ROWS = 16
CHUNK = 256


def prologue_kernel(lengths, tokens, gain, router, routes_t, normed, order):
    v = tokens[...].astype(F32)
    scale_rows = lax.rsqrt(jnp.mean(v * v, axis=-1, keepdims=True) + 1e-06)
    out = (v * scale_rows * gain[...]).astype(BF16)
    rows, width = out.shape
    normed[GATE_ROWS:, :] = out
    logits_t = lax.dot_general(router[...], out, (((1,), (1,)), ((), ())), preferred_element_type=F32)
    ids = lax.broadcasted_iota(jnp.int32, logits_t.shape, 0)
    position = lax.axis_index("tensor") * rows + lax.broadcasted_iota(jnp.int32, logits_t.shape, 1)
    named = routes_t[0:1, :] == ids
    for k in range(1, routes_t.shape[0]):
        named = named | (routes_t[k : k + 1, :] == ids)
    living = position < lengths[0]
    gates = jnp.where(named & living, jax.nn.sigmoid(logits_t), 0.0)
    high = gates.astype(BF16)
    normed[:GATE_ROWS, :rows] = high
    normed[:GATE_ROWS, rows : 2 * rows] = (gates - high.astype(F32)).astype(BF16)
    normed[:GATE_ROWS, 2 * rows :] = jnp.zeros((GATE_ROWS, width - 2 * rows), BF16)
    order[...] = jnp.zeros_like(order)


def pack_kernel(gate, up, down, *refs):
    packed, sems = refs[:-1], refs[-1]
    half = gate.shape[0]
    copies = []
    for h, chunk in enumerate(packed):
        units = pl.ds(CHUNK * h, CHUNK)
        copies.append((gate.at[:, units], chunk.at[:, pl.ds(0, CHUNK)]))
        copies.append((up.at[:, units], chunk.at[:, pl.ds(CHUNK, CHUNK)]))
        for i in range(half // CHUNK):
            columns = pl.ds(CHUNK * i, CHUNK)
            copies.append((down.at[units, columns], chunk.at[columns, pl.ds(2 * CHUNK, CHUNK)]))
    copies = [pltpu.make_async_copy(source, target, sems.at[i]) for i, (source, target) in enumerate(copies)]
    for copy in copies:
        copy.start()
    for copy in copies:
        copy.wait()


def expert_kernel(work, based, count, _, *refs):
    blocks, refs = refs[:count], refs[count:]
    bases, refs = (refs[: len(based)], refs[len(based) :])
    used = 4 * len(work)
    weights, refs = refs[:used], refs[used:]
    outs, (taken, weight, hidden, held, arrived) = refs[:count], refs[count:]
    rows, width = outs[0].shape
    half = width // 2
    x = lax.axis_index("dp")
    t = lax.axis_index("tensor")
    starts = (pl.multiple_of(x * half, half), pl.multiple_of((1 - x) * half, half))
    copies = [pltpu.make_async_copy(weights[i], held.at[i], arrived.at[i]) for i in range(used)]
    for copy in copies:
        copy.start()

    eye = lax.broadcasted_iota(jnp.int32, (rows, rows), 0) == lax.broadcasted_iota(jnp.int32, (rows, rows), 1)
    for b in range(count):
        here = pl.ds(b * rows, rows)
        taken[here, :] = blocks[b][GATE_ROWS:, :]
        lines = blocks[b][:GATE_ROWS, :rows].astype(F32) + blocks[b][:GATE_ROWS, rows : 2 * rows].astype(F32)
        ids = lax.broadcasted_iota(jnp.int32, lines.shape, 0)
        for n, (expert, first, last) in enumerate(work):
            if first <= b < last:
                line = jnp.sum(jnp.where(ids == jnp.bitwise_xor(t, 2 * expert), lines, 0.0), axis=0, keepdims=True)
                weight[n, here, :] = jnp.sum(jnp.where(eye, line, 0.0), axis=1, keepdims=True)

    for n, (_, first, last) in enumerate(work):
        here = pl.ds(first * rows, (last - first) * rows)
        near, away = (taken[here, pl.ds(start, half)] for start in starts)
        for h in range(2):
            own, far = 4 * n + 2 * h, 4 * n + 2 * h + 1
            copies[own].wait()
            copies[far].wait()
            gate = dot(near, held[own, :, :CHUNK]) + dot(away, held[far, :, :CHUNK])
            up = dot(near, held[own, :, CHUNK : 2 * CHUNK]) + dot(away, held[far, :, CHUNK : 2 * CHUNK])
            units = slice(CHUNK * h, CHUNK * (h + 1))
            hidden[n, here, units] = (jax.nn.silu(gate) * up * weight[n, here, :]).astype(BF16)

    edges = sorted({0, count}.union(*({first, last} for _, first, last in work)))
    for begin, end in zip(edges[:-1], edges[1:]):
        here = pl.ds(begin * rows, (end - begin) * rows)
        for side in range(2):
            for i in range(half // CHUNK):
                columns = pl.ds(pl.multiple_of(starts[side] + CHUNK * i, CHUNK), CHUNK)
                value = sum(
                    dot(hidden[n, here, CHUNK * h : CHUNK * (h + 1)], held[4 * n + 2 * h + side, CHUNK * i : CHUNK * (i + 1), 2 * CHUNK :])
                    for n, (_, first, last) in enumerate(work)
                    if first <= begin < last
                    for h in range(2)
                )
                for b in range(begin, end):
                    part = value[(b - begin) * rows : (b - begin + 1) * rows]
                    if b in based:
                        part = part + bases[based.index(b)][:, columns].astype(F32)
                    outs[b][:, columns] = part.astype(BF16)


def lanes(tokens, lengths, routes, norm_gain, router, w_gate, w_up, w_down):
    rows, width = tokens.shape
    half = width // 2
    hid = w_gate.shape[2]

    def send(v, pairs):
        return lax.ppermute(v, "tensor", pairs)

    def across(v):
        return lax.ppermute(v, "dp", [(0, 1), (1, 0)])

    by_core, by_y, outer, skip = ([(i, i ^ bit) for i in range(16)] for bit in (1, 2, 4, 8))
    smem = pl.BlockSpec(memory_space=pltpu.SMEM)
    vmem = pl.BlockSpec(memory_space=pltpu.VMEM)
    anywhere = pl.BlockSpec(memory_space=pl.ANY)

    own = pl.pallas_call(
        pack_kernel,
        out_shape=(jax.ShapeDtypeStruct((half, half), BF16),) * (hid // CHUNK),
        in_specs=[anywhere] * 3,
        out_specs=(vmem,) * (hid // CHUNK),
        scratch_shapes=[pltpu.SemaphoreType.DMA((hid // CHUNK * (2 + half // CHUNK),))],
        name="pack",
    )(w_gate[0], w_up[0], w_down[0])
    x_0 = across(own[0])
    y_1 = send(own[1], by_y)
    s_0, begin = pl.pallas_call(
        prologue_kernel,
        out_shape=(jax.ShapeDtypeStruct((rows + GATE_ROWS, width), BF16), jax.ShapeDtypeStruct((8, 128), F32)),
        in_specs=[smem] + [vmem] * 4,
        out_specs=(vmem,) * 2,
        name="prologue",
    )(lengths, tokens, norm_gain.reshape(1, width), router.T, routes.T)

    order = [begin]

    def together(*values):
        *values, order[0] = lax.optimization_barrier((*values, order[0]))
        return values

    def run(shards, work, bases):
        count = len(shards)
        based = tuple(b for b, base in enumerate(bases) if base is not None)
        used = 4 * len(work)
        return pl.pallas_call(
            functools.partial(expert_kernel, tuple((e, first, last) for e, _, first, last in work), based, count),
            out_shape=tuple(jax.ShapeDtypeStruct((rows, width), BF16) for _ in shards),
            in_specs=[anywhere] + [vmem] * (count + len(based)) + [anywhere] * used,
            out_specs=(vmem,) * count,
            scratch_shapes=[
                pltpu.VMEM((count * rows, width), BF16),
                pltpu.VMEM((len(work), count * rows, 1), F32),
                pltpu.VMEM((len(work), count * rows, 2 * CHUNK), BF16),
                pltpu.VMEM((used, half, half), BF16),
                pltpu.SemaphoreType.DMA((used,)),
            ],
            compiler_params=pltpu.CompilerParams(vmem_limit_bytes=36 * 2**20),
            cost_estimate=pl.CostEstimate(flops=1, bytes_accessed=1, transcendentals=0),
            name="experts",
        )(order[0], *shards, *(bases[b] for b in based), *(w for _, ws, _, _ in work for w in ws))

    def add(*terms):
        return sum(v.astype(F32) for v in terms).astype(BF16)

    s_a = send(s_0, outer)
    s_b = send(s_0, skip)
    m_0 = send(s_0, by_core)
    x_0, y_1, own_0, own_1 = together(x_0, y_1, *own)
    x_1 = across(own_1)
    y_0 = send(own_0, by_y)
    s_a, m_0 = together(s_a, m_0)
    s_b, s_a = together(s_b, s_a)
    s_c = send(s_b, outer)
    m_a, m_b = send(s_a, by_core), send(s_b, by_core)
    x_1, y_0, x_0, y_1 = together(x_1, y_0, x_0, y_1)
    d_0 = send(x_0, by_y)
    d_1 = across(y_1)
    mine = (own[0], x_0, own[1], x_1)
    m_a, m_b = together(m_a, m_b)
    u_0, v_0, u_a, v_a, u_b, v_b = run((s_0, m_0, s_a, m_a, s_b, m_b), [(0, mine, 0, 6)], [None] * 6)
    s_c, u_0, v_0, u_a, v_a, u_b, v_b = together(s_c, u_0, v_0, u_a, v_a, u_b, v_b)
    m_c = send(s_c, by_core)
    (m_c,) = together(m_c)
    u_c, v_c = run((s_c, m_c), [(0, mine, 0, 2)], [None] * 2)
    d_0, d_1, u_c, v_c = together(d_0, d_1, u_c, v_c)
    theirs = (y_0, d_0, y_1, d_1)
    p_c, o_c = run((s_c, m_c), [(1, theirs, 0, 2)], [u_c, v_c])
    r_c = send(o_c, by_core)

    r_c, p_c = together(r_c, p_c)
    r_n = send(add(p_c, r_c), outer)
    p_b, o_b, p_a, o_a, p_0, o_0 = run((s_b, m_b, s_a, m_a, s_0, m_0), [(1, theirs, 0, 6)], [u_b, v_b, u_a, v_a, u_0, v_0])
    r_b, r_a, r_0 = send(o_b, by_core), send(o_a, by_core), send(o_0, by_core)
    r_n, p_a = lax.optimization_barrier((r_n, p_a))
    r_b, r_a, p_b, r_n = lax.optimization_barrier((r_b, r_a, p_b, r_n))
    r_o = send(add(p_a, r_a), outer)
    r_m = send(add(p_b, r_b, r_n), skip)
    order[0] = p_0
    (r_o,) = together(r_o)
    (r_m,) = together(r_m)
    return add(tokens, order[0], r_0, r_o, r_m)


def solution(mesh):
    placed = (
        P(("dp", "tensor"), None),
        P("dp"),
        P(("dp", "tensor"), None),
        P(),
        P(),
        P("tensor", "dp", None),
        P("tensor", "dp", None),
        P("tensor", None, "dp"),
    )

    def shards(*args):
        fits = mesh.shape["dp"] == 2 and mesh.shape["tensor"] == 16 and args[5].shape[0] == 1
        fits = fits and args[1].shape[0] == 1 and args[0].shape[0] == 256 and args[4].shape[1] == GATE_ROWS
        fits = fits and args[5].shape[2] == 512 and args[0].shape[1] == 1536
        return (lanes if fits else general)(*args)

    return jax.shard_map(
        shards, mesh=mesh, in_specs=placed, out_specs=P(("dp", "tensor"), None), check_vma=False
    )
```

```python
import functools
import jax
import jax.numpy as jnp
from jax import lax
from jax.experimental import pallas as pl
from jax.experimental.pallas import tpu as pltpu
from jax.sharding import PartitionSpec as P

LMAX = 4096
F32 = jnp.float32
BF16 = jnp.bfloat16


def gate_of(logits, routes, lengths, experts):
    rows = logits.shape[0]
    position = lax.axis_index("tensor") * rows + jnp.arange(rows, dtype=jnp.int32)
    living = position % LMAX < lengths[position // LMAX]
    ids = jnp.arange(experts, dtype=jnp.int32)
    named = jnp.zeros((rows, experts), jnp.bool_)
    for k in range(routes.shape[1]):
        named = named | (routes[:, k : k + 1] == ids[None, :])
    return jnp.where(named & living[:, None], jax.nn.sigmoid(logits), 0.0)


def norm_of(tokens_f32, norm_gain):
    scale_rows = lax.rsqrt(jnp.mean(tokens_f32 * tokens_f32, axis=-1, keepdims=True) + 1e-06)
    return (tokens_f32 * scale_rows * norm_gain).astype(BF16)


def dot(a, b):
    return jnp.dot(a, b, preferred_element_type=F32)


def general(tokens, lengths, routes, norm_gain, router, w_gate, w_up, w_down):
    experts = router.shape[1]
    local = w_gate.shape[0]
    tokens_f32 = tokens.astype(F32)
    normed = norm_of(tokens_f32, norm_gain)
    gates = gate_of(dot(normed, router), routes, lengths, experts)
    gate_all = lax.all_gather(w_gate, "dp", axis=1, tiled=True)
    up_all = lax.all_gather(w_up, "dp", axis=1, tiled=True)
    down_all = lax.all_gather(w_down, "dp", axis=2, tiled=True)
    rows_all = lax.all_gather(normed, "tensor", axis=0, tiled=True)
    gates_all = lax.all_gather(gates, "tensor", axis=0, tiled=True)
    first = lax.axis_index("tensor") * local
    total = jnp.zeros(rows_all.shape, F32)
    for x in range(local):
        weight = lax.dynamic_slice_in_dim(gates_all, first + x, 1, axis=1)
        hidden = jax.nn.silu(dot(rows_all, gate_all[x])) * dot(rows_all, up_all[x])
        total = total + dot((hidden * weight).astype(BF16), down_all[x])
    combined = lax.psum_scatter(total.astype(BF16), "tensor", scatter_dimension=0, tiled=True)
    return (tokens_f32 + combined.astype(F32)).astype(BF16)


GATE_ROWS = 16
CHUNK = 256


def prologue_kernel(lengths, tokens, gain, router, routes_t, normed, order):
    v = tokens[...].astype(F32)
    scale_rows = lax.rsqrt(jnp.mean(v * v, axis=-1, keepdims=True) + 1e-06)
    out = (v * scale_rows * gain[...]).astype(BF16)
    rows, width = out.shape
    normed[GATE_ROWS:, :] = out
    logits_t = lax.dot_general(router[...], out, (((1,), (1,)), ((), ())), preferred_element_type=F32)
    ids = lax.broadcasted_iota(jnp.int32, logits_t.shape, 0)
    position = lax.axis_index("tensor") * rows + lax.broadcasted_iota(jnp.int32, logits_t.shape, 1)
    named = routes_t[0:1, :] == ids
    for k in range(1, routes_t.shape[0]):
        named = named | (routes_t[k : k + 1, :] == ids)
    living = position < lengths[0]
    gates = jnp.where(named & living, jax.nn.sigmoid(logits_t), 0.0)
    high = gates.astype(BF16)
    normed[:GATE_ROWS, :rows] = high
    normed[:GATE_ROWS, rows : 2 * rows] = (gates - high.astype(F32)).astype(BF16)
    normed[:GATE_ROWS, 2 * rows :] = jnp.zeros((GATE_ROWS, width - 2 * rows), BF16)
    order[...] = jnp.zeros_like(order)


def pack_kernel(gate, up, down, *refs):
    packed, sems = refs[:-1], refs[-1]
    half = gate.shape[0]
    copies = []
    for h, chunk in enumerate(packed):
        units = pl.ds(CHUNK * h, CHUNK)
        copies.append((gate.at[:, units], chunk.at[:, pl.ds(0, CHUNK)]))
        copies.append((up.at[:, units], chunk.at[:, pl.ds(CHUNK, CHUNK)]))
        for i in range(half // CHUNK):
            columns = pl.ds(CHUNK * i, CHUNK)
            copies.append((down.at[units, columns], chunk.at[columns, pl.ds(2 * CHUNK, CHUNK)]))
    copies = [pltpu.make_async_copy(source, target, sems.at[i]) for i, (source, target) in enumerate(copies)]
    for copy in copies:
        copy.start()
    for copy in copies:
        copy.wait()


def expert_kernel(work, based, count, _, *refs):
    blocks, refs = refs[:count], refs[count:]
    bases, refs = (refs[: len(based)], refs[len(based) :])
    used = 4 * len(work)
    weights, refs = refs[:used], refs[used:]
    outs, (taken, weight, hidden, held, arrived) = refs[:count], refs[count:]
    rows, width = outs[0].shape
    half = width // 2
    x = lax.axis_index("dp")
    t = lax.axis_index("tensor")
    starts = (pl.multiple_of(x * half, half), pl.multiple_of((1 - x) * half, half))
    copies = [pltpu.make_async_copy(weights[i], held.at[i], arrived.at[i]) for i in range(used)]
    for copy in copies:
        copy.start()

    eye = lax.broadcasted_iota(jnp.int32, (rows, rows), 0) == lax.broadcasted_iota(jnp.int32, (rows, rows), 1)
    for b in range(count):
        here = pl.ds(b * rows, rows)
        taken[here, :] = blocks[b][GATE_ROWS:, :]
        lines = blocks[b][:GATE_ROWS, :rows].astype(F32) + blocks[b][:GATE_ROWS, rows : 2 * rows].astype(F32)
        ids = lax.broadcasted_iota(jnp.int32, lines.shape, 0)
        for n, (expert, first, last) in enumerate(work):
            if first <= b < last:
                line = jnp.sum(jnp.where(ids == jnp.bitwise_xor(t, 2 * expert), lines, 0.0), axis=0, keepdims=True)
                weight[n, here, :] = jnp.sum(jnp.where(eye, line, 0.0), axis=1, keepdims=True)

    for n, (_, first, last) in enumerate(work):
        here = pl.ds(first * rows, (last - first) * rows)
        near, away = (taken[here, pl.ds(start, half)] for start in starts)
        for h in range(2):
            own, far = 4 * n + 2 * h, 4 * n + 2 * h + 1
            copies[own].wait()
            copies[far].wait()
            gate = dot(near, held[own, :, :CHUNK]) + dot(away, held[far, :, :CHUNK])
            up = dot(near, held[own, :, CHUNK : 2 * CHUNK]) + dot(away, held[far, :, CHUNK : 2 * CHUNK])
            units = slice(CHUNK * h, CHUNK * (h + 1))
            hidden[n, here, units] = (jax.nn.silu(gate) * up * weight[n, here, :]).astype(BF16)

    edges = sorted({0, count}.union(*({first, last} for _, first, last in work)))
    for begin, end in zip(edges[:-1], edges[1:]):
        here = pl.ds(begin * rows, (end - begin) * rows)
        for side in range(2):
            for i in range(half // CHUNK):
                columns = pl.ds(pl.multiple_of(starts[side] + CHUNK * i, CHUNK), CHUNK)
                value = sum(
                    dot(hidden[n, here, CHUNK * h : CHUNK * (h + 1)], held[4 * n + 2 * h + side, CHUNK * i : CHUNK * (i + 1), 2 * CHUNK :])
                    for n, (_, first, last) in enumerate(work)
                    if first <= begin < last
                    for h in range(2)
                )
                for b in range(begin, end):
                    part = value[(b - begin) * rows : (b - begin + 1) * rows]
                    if b in based:
                        part = part + bases[based.index(b)][:, columns].astype(F32)
                    outs[b][:, columns] = part.astype(BF16)


def lanes(tokens, lengths, routes, norm_gain, router, w_gate, w_up, w_down):
    rows, width = tokens.shape
    half = width // 2
    hid = w_gate.shape[2]

    def send(v, pairs):
        return lax.ppermute(v, "tensor", pairs)

    def across(v):
        return lax.ppermute(v, "dp", [(0, 1), (1, 0)])

    by_core, by_y, outer, skip = ([(i, i ^ bit) for i in range(16)] for bit in (1, 2, 4, 8))
    smem = pl.BlockSpec(memory_space=pltpu.SMEM)
    vmem = pl.BlockSpec(memory_space=pltpu.VMEM)
    anywhere = pl.BlockSpec(memory_space=pl.ANY)

    own = pl.pallas_call(
        pack_kernel,
        out_shape=(jax.ShapeDtypeStruct((half, half), BF16),) * (hid // CHUNK),
        in_specs=[anywhere] * 3,
        out_specs=(vmem,) * (hid // CHUNK),
        scratch_shapes=[pltpu.SemaphoreType.DMA((hid // CHUNK * (2 + half // CHUNK),))],
        name="pack",
    )(w_gate[0], w_up[0], w_down[0])
    x_0 = across(own[0])
    y_1 = send(own[1], by_y)
    s_0, begin = pl.pallas_call(
        prologue_kernel,
        out_shape=(jax.ShapeDtypeStruct((rows + GATE_ROWS, width), BF16), jax.ShapeDtypeStruct((8, 128), F32)),
        in_specs=[smem] + [vmem] * 4,
        out_specs=(vmem,) * 2,
        name="prologue",
    )(lengths, tokens, norm_gain.reshape(1, width), router.T, routes.T)

    order = [begin]

    def together(*values):
        *values, order[0] = lax.optimization_barrier((*values, order[0]))
        return values

    def run(shards, work, bases):
        count = len(shards)
        based = tuple(b for b, base in enumerate(bases) if base is not None)
        used = 4 * len(work)
        return pl.pallas_call(
            functools.partial(expert_kernel, tuple((e, first, last) for e, _, first, last in work), based, count),
            out_shape=tuple(jax.ShapeDtypeStruct((rows, width), BF16) for _ in shards),
            in_specs=[anywhere] + [vmem] * (count + len(based)) + [anywhere] * used,
            out_specs=(vmem,) * count,
            scratch_shapes=[
                pltpu.VMEM((count * rows, width), BF16),
                pltpu.VMEM((len(work), count * rows, 1), F32),
                pltpu.VMEM((len(work), count * rows, 2 * CHUNK), BF16),
                pltpu.VMEM((used, half, half), BF16),
                pltpu.SemaphoreType.DMA((used,)),
            ],
            compiler_params=pltpu.CompilerParams(vmem_limit_bytes=36 * 2**20),
            cost_estimate=pl.CostEstimate(flops=1, bytes_accessed=1, transcendentals=0),
            name="experts",
        )(order[0], *shards, *(bases[b] for b in based), *(w for _, ws, _, _ in work for w in ws))

    def add(*terms):
        return sum(v.astype(F32) for v in terms).astype(BF16)

    s_a = send(s_0, outer)
    s_b = send(s_0, skip)
    m_0 = send(s_0, by_core)
    x_0, y_1, own_0, own_1 = together(x_0, y_1, *own)
    x_1 = across(own_1)
    y_0 = send(own_0, by_y)
    s_a, m_0 = together(s_a, m_0)
    s_b, s_a = together(s_b, s_a)
    s_c = send(s_b, outer)
    m_a, m_b = send(s_a, by_core), send(s_b, by_core)
    m_a, m_b, x_0, y_1 = together(m_a, m_b, x_0, y_1)
    d_0 = send(x_0, by_y)
    d_1 = across(y_1)
    x_1, y_0 = together(x_1, y_0)
    mine = (own[0], x_0, own[1], x_1)
    u_0, v_0, u_a, v_a, u_b, v_b = run((s_0, m_0, s_a, m_a, s_b, m_b), [(0, mine, 0, 6)], [None] * 6)
    s_c, u_0, v_0, u_a, v_a, u_b, v_b = together(s_c, u_0, v_0, u_a, v_a, u_b, v_b)
    m_c = send(s_c, by_core)
    (m_c,) = together(m_c)
    u_c, v_c = run((s_c, m_c), [(0, mine, 0, 2)], [None] * 2)
    d_0, d_1, u_c, v_c = together(d_0, d_1, u_c, v_c)
    theirs = (y_0, d_0, y_1, d_1)
    p_c, o_c = run((s_c, m_c), [(1, theirs, 0, 2)], [u_c, v_c])
    r_c = send(o_c, by_core)

    r_c, p_c = together(r_c, p_c)
    r_n = send(add(p_c, r_c), outer)
    p_b, o_b, p_a, o_a, p_0, o_0 = run((s_b, m_b, s_a, m_a, s_0, m_0), [(1, theirs, 0, 6)], [u_b, v_b, u_a, v_a, u_0, v_0])
    r_b, r_a, r_0 = send(o_b, by_core), send(o_a, by_core), send(o_0, by_core)
    r_n, p_a = lax.optimization_barrier((r_n, p_a))
    r_b, r_a, p_b, r_n = lax.optimization_barrier((r_b, r_a, p_b, r_n))
    r_o = send(add(p_a, r_a), outer)
    r_m = send(add(p_b, r_b, r_n), skip)
    order[0] = p_0
    (r_o,) = together(r_o)
    (r_m,) = together(r_m)
    return add(tokens, order[0], r_0, r_o, r_m)


def solution(mesh):
    placed = (
        P(("dp", "tensor"), None),
        P("dp"),
        P(("dp", "tensor"), None),
        P(),
        P(),
        P("tensor", "dp", None),
        P("tensor", "dp", None),
        P("tensor", None, "dp"),
    )

    def shards(*args):
        fits = mesh.shape["dp"] == 2 and mesh.shape["tensor"] == 16 and args[5].shape[0] == 1
        fits = fits and args[1].shape[0] == 1 and args[0].shape[0] == 256 and args[4].shape[1] == GATE_ROWS
        fits = fits and args[5].shape[2] == 512 and args[0].shape[1] == 1536
        return (lanes if fits else general)(*args)

    return jax.shard_map(
        shards, mesh=mesh, in_specs=placed, out_specs=P(("dp", "tensor"), None), check_vma=False
    )
```

```python
import functools
import jax
import jax.numpy as jnp
from jax import lax
from jax.experimental import pallas as pl
from jax.experimental.pallas import tpu as pltpu
from jax.sharding import PartitionSpec as P

LMAX = 4096
F32 = jnp.float32
BF16 = jnp.bfloat16


def gate_of(logits, routes, lengths, experts):
    rows = logits.shape[0]
    position = lax.axis_index("tensor") * rows + jnp.arange(rows, dtype=jnp.int32)
    living = position % LMAX < lengths[position // LMAX]
    ids = jnp.arange(experts, dtype=jnp.int32)
    named = jnp.zeros((rows, experts), jnp.bool_)
    for k in range(routes.shape[1]):
        named = named | (routes[:, k : k + 1] == ids[None, :])
    return jnp.where(named & living[:, None], jax.nn.sigmoid(logits), 0.0)


def norm_of(tokens_f32, norm_gain):
    scale_rows = lax.rsqrt(jnp.mean(tokens_f32 * tokens_f32, axis=-1, keepdims=True) + 1e-06)
    return (tokens_f32 * scale_rows * norm_gain).astype(BF16)


def dot(a, b):
    return jnp.dot(a, b, preferred_element_type=F32)


def general(tokens, lengths, routes, norm_gain, router, w_gate, w_up, w_down):
    experts = router.shape[1]
    local = w_gate.shape[0]
    tokens_f32 = tokens.astype(F32)
    normed = norm_of(tokens_f32, norm_gain)
    gates = gate_of(dot(normed, router), routes, lengths, experts)
    gate_all = lax.all_gather(w_gate, "dp", axis=1, tiled=True)
    up_all = lax.all_gather(w_up, "dp", axis=1, tiled=True)
    down_all = lax.all_gather(w_down, "dp", axis=2, tiled=True)
    rows_all = lax.all_gather(normed, "tensor", axis=0, tiled=True)
    gates_all = lax.all_gather(gates, "tensor", axis=0, tiled=True)
    first = lax.axis_index("tensor") * local
    total = jnp.zeros(rows_all.shape, F32)
    for x in range(local):
        weight = lax.dynamic_slice_in_dim(gates_all, first + x, 1, axis=1)
        hidden = jax.nn.silu(dot(rows_all, gate_all[x])) * dot(rows_all, up_all[x])
        total = total + dot((hidden * weight).astype(BF16), down_all[x])
    combined = lax.psum_scatter(total.astype(BF16), "tensor", scatter_dimension=0, tiled=True)
    return (tokens_f32 + combined.astype(F32)).astype(BF16)


GATE_ROWS = 16
CHUNK = 256


def prologue_kernel(lengths, tokens, gain, router, routes_t, normed, order):
    v = tokens[...].astype(F32)
    scale_rows = lax.rsqrt(jnp.mean(v * v, axis=-1, keepdims=True) + 1e-06)
    out = (v * scale_rows * gain[...]).astype(BF16)
    rows, width = out.shape
    normed[GATE_ROWS:, :] = out
    logits_t = lax.dot_general(router[...], out, (((1,), (1,)), ((), ())), preferred_element_type=F32)
    ids = lax.broadcasted_iota(jnp.int32, logits_t.shape, 0)
    position = lax.axis_index("tensor") * rows + lax.broadcasted_iota(jnp.int32, logits_t.shape, 1)
    named = routes_t[0:1, :] == ids
    for k in range(1, routes_t.shape[0]):
        named = named | (routes_t[k : k + 1, :] == ids)
    living = position < lengths[0]
    gates = jnp.where(named & living, jax.nn.sigmoid(logits_t), 0.0)
    high = gates.astype(BF16)
    normed[:GATE_ROWS, :rows] = high
    normed[:GATE_ROWS, rows : 2 * rows] = (gates - high.astype(F32)).astype(BF16)
    normed[:GATE_ROWS, 2 * rows :] = jnp.zeros((GATE_ROWS, width - 2 * rows), BF16)
    order[...] = jnp.zeros_like(order)


def pack_kernel(gate, up, down, *refs):
    packed, sems = refs[:-1], refs[-1]
    half = gate.shape[0]
    copies = []
    for h, chunk in enumerate(packed):
        units = pl.ds(CHUNK * h, CHUNK)
        copies.append((gate.at[:, units], chunk.at[:, pl.ds(0, CHUNK)]))
        copies.append((up.at[:, units], chunk.at[:, pl.ds(CHUNK, CHUNK)]))
        for i in range(half // CHUNK):
            columns = pl.ds(CHUNK * i, CHUNK)
            copies.append((down.at[units, columns], chunk.at[columns, pl.ds(2 * CHUNK, CHUNK)]))
    copies = [pltpu.make_async_copy(source, target, sems.at[i]) for i, (source, target) in enumerate(copies)]
    for copy in copies:
        copy.start()
    for copy in copies:
        copy.wait()


def expert_kernel(work, based, count, _, *refs):
    blocks, refs = refs[:count], refs[count:]
    bases, refs = (refs[: len(based)], refs[len(based) :])
    used = 4 * len(work)
    weights, refs = refs[:used], refs[used:]
    outs, (taken, weight, hidden, held, arrived) = refs[:count], refs[count:]
    rows, width = outs[0].shape
    half = width // 2
    x = lax.axis_index("dp")
    t = lax.axis_index("tensor")
    starts = (pl.multiple_of(x * half, half), pl.multiple_of((1 - x) * half, half))
    copies = [pltpu.make_async_copy(weights[i], held.at[i], arrived.at[i]) for i in range(used)]
    for copy in copies:
        copy.start()

    eye = lax.broadcasted_iota(jnp.int32, (rows, rows), 0) == lax.broadcasted_iota(jnp.int32, (rows, rows), 1)
    for b in range(count):
        here = pl.ds(b * rows, rows)
        taken[here, :] = blocks[b][GATE_ROWS:, :]
        lines = blocks[b][:GATE_ROWS, :rows].astype(F32) + blocks[b][:GATE_ROWS, rows : 2 * rows].astype(F32)
        ids = lax.broadcasted_iota(jnp.int32, lines.shape, 0)
        for n, (expert, first, last) in enumerate(work):
            if first <= b < last:
                line = jnp.sum(jnp.where(ids == jnp.bitwise_xor(t, 2 * expert), lines, 0.0), axis=0, keepdims=True)
                weight[n, here, :] = jnp.sum(jnp.where(eye, line, 0.0), axis=1, keepdims=True)

    for n, (_, first, last) in enumerate(work):
        here = pl.ds(first * rows, (last - first) * rows)
        near, away = (taken[here, pl.ds(start, half)] for start in starts)
        for h in range(2):
            own, far = 4 * n + 2 * h, 4 * n + 2 * h + 1
            copies[own].wait()
            copies[far].wait()
            gate = dot(near, held[own, :, :CHUNK]) + dot(away, held[far, :, :CHUNK])
            up = dot(near, held[own, :, CHUNK : 2 * CHUNK]) + dot(away, held[far, :, CHUNK : 2 * CHUNK])
            units = slice(CHUNK * h, CHUNK * (h + 1))
            hidden[n, here, units] = (jax.nn.silu(gate) * up * weight[n, here, :]).astype(BF16)

    edges = sorted({0, count}.union(*({first, last} for _, first, last in work)))
    for begin, end in zip(edges[:-1], edges[1:]):
        here = pl.ds(begin * rows, (end - begin) * rows)
        for side in range(2):
            for i in range(half // CHUNK):
                columns = pl.ds(pl.multiple_of(starts[side] + CHUNK * i, CHUNK), CHUNK)
                value = sum(
                    dot(hidden[n, here, CHUNK * h : CHUNK * (h + 1)], held[4 * n + 2 * h + side, CHUNK * i : CHUNK * (i + 1), 2 * CHUNK :])
                    for n, (_, first, last) in enumerate(work)
                    if first <= begin < last
                    for h in range(2)
                )
                for b in range(begin, end):
                    part = value[(b - begin) * rows : (b - begin + 1) * rows]
                    if b in based:
                        part = part + bases[based.index(b)][:, columns].astype(F32)
                    outs[b][:, columns] = part.astype(BF16)


def lanes(tokens, lengths, routes, norm_gain, router, w_gate, w_up, w_down):
    rows, width = tokens.shape
    half = width // 2
    hid = w_gate.shape[2]

    def send(v, pairs):
        return lax.ppermute(v, "tensor", pairs)

    def across(v):
        return lax.ppermute(v, "dp", [(0, 1), (1, 0)])

    by_core, by_y, outer, skip = ([(i, i ^ bit) for i in range(16)] for bit in (1, 2, 4, 8))
    smem = pl.BlockSpec(memory_space=pltpu.SMEM)
    vmem = pl.BlockSpec(memory_space=pltpu.VMEM)
    anywhere = pl.BlockSpec(memory_space=pl.ANY)

    own = pl.pallas_call(
        pack_kernel,
        out_shape=(jax.ShapeDtypeStruct((half, half), BF16),) * (hid // CHUNK),
        in_specs=[anywhere] * 3,
        out_specs=(vmem,) * (hid // CHUNK),
        scratch_shapes=[pltpu.SemaphoreType.DMA((hid // CHUNK * (2 + half // CHUNK),))],
        name="pack",
    )(w_gate[0], w_up[0], w_down[0])
    x_0 = across(own[0])
    y_1 = send(own[1], by_y)
    s_0, begin = pl.pallas_call(
        prologue_kernel,
        out_shape=(jax.ShapeDtypeStruct((rows + GATE_ROWS, width), BF16), jax.ShapeDtypeStruct((8, 128), F32)),
        in_specs=[smem] + [vmem] * 4,
        out_specs=(vmem,) * 2,
        name="prologue",
    )(lengths, tokens, norm_gain.reshape(1, width), router.T, routes.T)

    order = [begin]

    def together(*values):
        *values, order[0] = lax.optimization_barrier((*values, order[0]))
        return values

    def run(shards, work, bases):
        count = len(shards)
        based = tuple(b for b, base in enumerate(bases) if base is not None)
        used = 4 * len(work)
        return pl.pallas_call(
            functools.partial(expert_kernel, tuple((e, first, last) for e, _, first, last in work), based, count),
            out_shape=tuple(jax.ShapeDtypeStruct((rows, width), BF16) for _ in shards),
            in_specs=[anywhere] + [vmem] * (count + len(based)) + [anywhere] * used,
            out_specs=(vmem,) * count,
            scratch_shapes=[
                pltpu.VMEM((count * rows, width), BF16),
                pltpu.VMEM((len(work), count * rows, 1), F32),
                pltpu.VMEM((len(work), count * rows, 2 * CHUNK), BF16),
                pltpu.VMEM((used, half, half), BF16),
                pltpu.SemaphoreType.DMA((used,)),
            ],
            compiler_params=pltpu.CompilerParams(vmem_limit_bytes=36 * 2**20),
            cost_estimate=pl.CostEstimate(flops=1, bytes_accessed=1, transcendentals=0),
            name="experts",
        )(order[0], *shards, *(bases[b] for b in based), *(w for _, ws, _, _ in work for w in ws))

    def add(*terms):
        return sum(v.astype(F32) for v in terms).astype(BF16)

    s_a = send(s_0, outer)
    s_b = send(s_0, skip)
    m_0 = send(s_0, by_core)
    x_0, y_1, own_0, own_1 = together(x_0, y_1, *own)
    x_1 = across(own_1)
    y_0 = send(own_0, by_y)
    s_a, m_0 = together(s_a, m_0)
    s_b, s_a = together(s_b, s_a)
    s_c = send(s_b, outer)
    m_a, m_b = send(s_a, by_core), send(s_b, by_core)
    m_a, m_b, x_0, y_1 = together(m_a, m_b, x_0, y_1)
    d_0 = send(x_0, by_y)
    d_1 = across(y_1)
    x_1, y_0 = together(x_1, y_0)
    mine = (own[0], x_0, own[1], x_1)
    u_0, v_0, u_a, v_a, u_b, v_b = run((s_0, m_0, s_a, m_a, s_b, m_b), [(0, mine, 0, 6)], [None] * 6)
    s_c, u_0, v_0, u_a, v_a, u_b, v_b = together(s_c, u_0, v_0, u_a, v_a, u_b, v_b)
    m_c = send(s_c, by_core)
    (m_c,) = together(m_c)
    u_c, v_c = run((s_c, m_c), [(0, mine, 0, 2)], [None] * 2)
    d_0, d_1, u_c, v_c = together(d_0, d_1, u_c, v_c)
    theirs = (y_0, d_0, y_1, d_1)
    p_c, o_c = run((s_c, m_c), [(1, theirs, 0, 2)], [u_c, v_c])
    r_c = send(o_c, by_core)

    r_c, p_c = together(r_c, p_c)
    r_n = send(add(p_c, r_c), outer)
    p_b, o_b, p_a, o_a, p_0, o_0 = run((s_b, m_b, s_a, m_a, s_0, m_0), [(1, theirs, 0, 6)], [u_b, v_b, u_a, v_a, u_0, v_0])
    r_b, r_a, r_0 = send(o_b, by_core), send(o_a, by_core), send(o_0, by_core)
    r_n, p_a = lax.optimization_barrier((r_n, p_a))
    r_b, r_a, p_b, r_n = lax.optimization_barrier((r_b, r_a, p_b, r_n))
    r_o = send(add(p_a, r_a), outer)
    r_m = send(add(p_b, r_b, r_n), skip)
    order[0] = p_0
    (r_m,) = together(r_m)
    (r_o,) = together(r_o)
    return add(tokens, order[0], r_0, r_o, r_m)


def solution(mesh):
    placed = (
        P(("dp", "tensor"), None),
        P("dp"),
        P(("dp", "tensor"), None),
        P(),
        P(),
        P("tensor", "dp", None),
        P("tensor", "dp", None),
        P("tensor", None, "dp"),
    )

    def shards(*args):
        fits = mesh.shape["dp"] == 2 and mesh.shape["tensor"] == 16 and args[5].shape[0] == 1
        fits = fits and args[1].shape[0] == 1 and args[0].shape[0] == 256 and args[4].shape[1] == GATE_ROWS
        fits = fits and args[5].shape[2] == 512 and args[0].shape[1] == 1536
        return (lanes if fits else general)(*args)

    return jax.shard_map(
        shards, mesh=mesh, in_specs=placed, out_specs=P(("dp", "tensor"), None), check_vma=False
    )
```

```python
import functools
import jax
import jax.numpy as jnp
from jax import lax
from jax.experimental import pallas as pl
from jax.experimental.pallas import tpu as pltpu
from jax.sharding import PartitionSpec as P

LMAX = 4096
F32 = jnp.float32
BF16 = jnp.bfloat16


def gate_of(logits, routes, lengths, experts):
    rows = logits.shape[0]
    position = lax.axis_index("tensor") * rows + jnp.arange(rows, dtype=jnp.int32)
    living = position % LMAX < lengths[position // LMAX]
    ids = jnp.arange(experts, dtype=jnp.int32)
    named = jnp.zeros((rows, experts), jnp.bool_)
    for k in range(routes.shape[1]):
        named = named | (routes[:, k : k + 1] == ids[None, :])
    return jnp.where(named & living[:, None], jax.nn.sigmoid(logits), 0.0)


def norm_of(tokens_f32, norm_gain):
    scale_rows = lax.rsqrt(jnp.mean(tokens_f32 * tokens_f32, axis=-1, keepdims=True) + 1e-06)
    return (tokens_f32 * scale_rows * norm_gain).astype(BF16)


def dot(a, b):
    return jnp.dot(a, b, preferred_element_type=F32)


def general(tokens, lengths, routes, norm_gain, router, w_gate, w_up, w_down):
    experts = router.shape[1]
    local = w_gate.shape[0]
    tokens_f32 = tokens.astype(F32)
    normed = norm_of(tokens_f32, norm_gain)
    gates = gate_of(dot(normed, router), routes, lengths, experts)
    gate_all = lax.all_gather(w_gate, "dp", axis=1, tiled=True)
    up_all = lax.all_gather(w_up, "dp", axis=1, tiled=True)
    down_all = lax.all_gather(w_down, "dp", axis=2, tiled=True)
    rows_all = lax.all_gather(normed, "tensor", axis=0, tiled=True)
    gates_all = lax.all_gather(gates, "tensor", axis=0, tiled=True)
    first = lax.axis_index("tensor") * local
    total = jnp.zeros(rows_all.shape, F32)
    for x in range(local):
        weight = lax.dynamic_slice_in_dim(gates_all, first + x, 1, axis=1)
        hidden = jax.nn.silu(dot(rows_all, gate_all[x])) * dot(rows_all, up_all[x])
        total = total + dot((hidden * weight).astype(BF16), down_all[x])
    combined = lax.psum_scatter(total.astype(BF16), "tensor", scatter_dimension=0, tiled=True)
    return (tokens_f32 + combined.astype(F32)).astype(BF16)


GATE_ROWS = 16
CHUNK = 256


def prologue_kernel(lengths, tokens, gain, router, routes_t, normed, order):
    v = tokens[...].astype(F32)
    scale_rows = lax.rsqrt(jnp.mean(v * v, axis=-1, keepdims=True) + 1e-06)
    out = (v * scale_rows * gain[...]).astype(BF16)
    rows, width = out.shape
    normed[GATE_ROWS:, :] = out
    logits_t = lax.dot_general(router[...], out, (((1,), (1,)), ((), ())), preferred_element_type=F32)
    ids = lax.broadcasted_iota(jnp.int32, logits_t.shape, 0)
    position = lax.axis_index("tensor") * rows + lax.broadcasted_iota(jnp.int32, logits_t.shape, 1)
    named = routes_t[0:1, :] == ids
    for k in range(1, routes_t.shape[0]):
        named = named | (routes_t[k : k + 1, :] == ids)
    living = position < lengths[0]
    gates = jnp.where(named & living, jax.nn.sigmoid(logits_t), 0.0)
    high = gates.astype(BF16)
    normed[:GATE_ROWS, :rows] = high
    normed[:GATE_ROWS, rows : 2 * rows] = (gates - high.astype(F32)).astype(BF16)
    normed[:GATE_ROWS, 2 * rows :] = jnp.zeros((GATE_ROWS, width - 2 * rows), BF16)
    order[...] = jnp.zeros_like(order)


def pack_kernel(gate, up, down, *refs):
    chunks = len(refs) - 3
    packed, (held, arrived, left) = refs[:chunks], refs[chunks:]
    half = gate.shape[0]
    reads = []
    for h in range(chunks):
        units, chunk = pl.ds(CHUNK * h, CHUNK), held.at[h]
        pairs = [(gate.at[:, units], chunk.at[:, pl.ds(0, CHUNK)]), (up.at[:, units], chunk.at[:, pl.ds(CHUNK, CHUNK)])]
        for i in range(half // CHUNK):
            columns = pl.ds(CHUNK * i, CHUNK)
            pairs.append((down.at[units, columns], chunk.at[columns, pl.ds(2 * CHUNK, CHUNK)]))
        reads.append([pltpu.make_async_copy(source, target, arrived.at[h, i]) for i, (source, target) in enumerate(pairs)])
        for copy in reads[-1]:
            copy.start()
    writes = [pltpu.make_async_copy(held.at[h], packed[h], left.at[h]) for h in range(chunks)]
    for h in range(chunks):
        for copy in reads[h]:
            copy.wait()
        writes[h].start()
    for copy in writes:
        copy.wait()


def expert_kernel(work, based, count, _, *refs):
    blocks, refs = refs[:count], refs[count:]
    bases, refs = (refs[: len(based)], refs[len(based) :])
    used = 4 * len(work)
    weights, refs = refs[:used], refs[used:]
    outs, (taken, weight, hidden, held, arrived) = refs[:count], refs[count:]
    rows, width = outs[0].shape
    half = width // 2
    x = lax.axis_index("dp")
    t = lax.axis_index("tensor")
    starts = (pl.multiple_of(x * half, half), pl.multiple_of((1 - x) * half, half))
    copies = [pltpu.make_async_copy(weights[i], held.at[i], arrived.at[i]) for i in range(used)]
    for copy in copies:
        copy.start()

    eye = lax.broadcasted_iota(jnp.int32, (rows, rows), 0) == lax.broadcasted_iota(jnp.int32, (rows, rows), 1)
    for b in range(count):
        here = pl.ds(b * rows, rows)
        taken[here, :] = blocks[b][GATE_ROWS:, :]
        lines = blocks[b][:GATE_ROWS, :rows].astype(F32) + blocks[b][:GATE_ROWS, rows : 2 * rows].astype(F32)
        ids = lax.broadcasted_iota(jnp.int32, lines.shape, 0)
        for n, (expert, first, last) in enumerate(work):
            if first <= b < last:
                line = jnp.sum(jnp.where(ids == jnp.bitwise_xor(t, 2 * expert), lines, 0.0), axis=0, keepdims=True)
                weight[n, here, :] = jnp.sum(jnp.where(eye, line, 0.0), axis=1, keepdims=True)

    for n, (_, first, last) in enumerate(work):
        here = pl.ds(first * rows, (last - first) * rows)
        near, away = (taken[here, pl.ds(start, half)] for start in starts)
        for h in range(2):
            own, far = 4 * n + 2 * h, 4 * n + 2 * h + 1
            copies[own].wait()
            copies[far].wait()
            gate = dot(near, held[own, :, :CHUNK]) + dot(away, held[far, :, :CHUNK])
            up = dot(near, held[own, :, CHUNK : 2 * CHUNK]) + dot(away, held[far, :, CHUNK : 2 * CHUNK])
            units = slice(CHUNK * h, CHUNK * (h + 1))
            hidden[n, here, units] = (jax.nn.silu(gate) * up * weight[n, here, :]).astype(BF16)

    edges = sorted({0, count}.union(*({first, last} for _, first, last in work)))
    for begin, end in zip(edges[:-1], edges[1:]):
        here = pl.ds(begin * rows, (end - begin) * rows)
        for side in range(2):
            for i in range(half // CHUNK):
                columns = pl.ds(pl.multiple_of(starts[side] + CHUNK * i, CHUNK), CHUNK)
                value = sum(
                    dot(hidden[n, here, CHUNK * h : CHUNK * (h + 1)], held[4 * n + 2 * h + side, CHUNK * i : CHUNK * (i + 1), 2 * CHUNK :])
                    for n, (_, first, last) in enumerate(work)
                    if first <= begin < last
                    for h in range(2)
                )
                for b in range(begin, end):
                    part = value[(b - begin) * rows : (b - begin + 1) * rows]
                    if b in based:
                        part = part + bases[based.index(b)][:, columns].astype(F32)
                    outs[b][:, columns] = part.astype(BF16)


def lanes(tokens, lengths, routes, norm_gain, router, w_gate, w_up, w_down):
    rows, width = tokens.shape
    half = width // 2
    hid = w_gate.shape[2]

    def send(v, pairs):
        return lax.ppermute(v, "tensor", pairs)

    def across(v):
        return lax.ppermute(v, "dp", [(0, 1), (1, 0)])

    by_core, by_y, outer, skip = ([(i, i ^ bit) for i in range(16)] for bit in (1, 2, 4, 8))
    smem = pl.BlockSpec(memory_space=pltpu.SMEM)
    vmem = pl.BlockSpec(memory_space=pltpu.VMEM)
    anywhere = pl.BlockSpec(memory_space=pl.ANY)

    own = pl.pallas_call(
        pack_kernel,
        out_shape=(jax.ShapeDtypeStruct((half, half), BF16),) * (hid // CHUNK),
        in_specs=[anywhere] * 3,
        out_specs=(anywhere,) * (hid // CHUNK),
        scratch_shapes=[
            pltpu.VMEM((hid // CHUNK, half, half), BF16),
            pltpu.SemaphoreType.DMA((hid // CHUNK, 2 + half // CHUNK)),
            pltpu.SemaphoreType.DMA((hid // CHUNK,)),
        ],
        name="pack",
    )(w_gate[0], w_up[0], w_down[0])
    x_0 = across(own[0])
    y_1 = send(own[1], by_y)
    s_0, begin = pl.pallas_call(
        prologue_kernel,
        out_shape=(jax.ShapeDtypeStruct((rows + GATE_ROWS, width), BF16), jax.ShapeDtypeStruct((8, 128), F32)),
        in_specs=[smem] + [vmem] * 4,
        out_specs=(vmem,) * 2,
        name="prologue",
    )(lengths, tokens, norm_gain.reshape(1, width), router.T, routes.T)

    order = [begin]

    def together(*values):
        *values, order[0] = lax.optimization_barrier((*values, order[0]))
        return values

    def run(shards, work, bases):
        count = len(shards)
        based = tuple(b for b, base in enumerate(bases) if base is not None)
        used = 4 * len(work)
        return pl.pallas_call(
            functools.partial(expert_kernel, tuple((e, first, last) for e, _, first, last in work), based, count),
            out_shape=tuple(jax.ShapeDtypeStruct((rows, width), BF16) for _ in shards),
            in_specs=[anywhere] + [vmem] * (count + len(based)) + [anywhere] * used,
            out_specs=(vmem,) * count,
            scratch_shapes=[
                pltpu.VMEM((count * rows, width), BF16),
                pltpu.VMEM((len(work), count * rows, 1), F32),
                pltpu.VMEM((len(work), count * rows, 2 * CHUNK), BF16),
                pltpu.VMEM((used, half, half), BF16),
                pltpu.SemaphoreType.DMA((used,)),
            ],
            compiler_params=pltpu.CompilerParams(vmem_limit_bytes=36 * 2**20),
            cost_estimate=pl.CostEstimate(flops=1, bytes_accessed=1, transcendentals=0),
            name="experts",
        )(order[0], *shards, *(bases[b] for b in based), *(w for _, ws, _, _ in work for w in ws))

    def add(*terms):
        return sum(v.astype(F32) for v in terms).astype(BF16)

    s_a = send(s_0, outer)
    s_b = send(s_0, skip)
    m_0 = send(s_0, by_core)
    x_0, y_1, own_0, own_1 = together(x_0, y_1, *own)
    x_1 = across(own_1)
    y_0 = send(own_0, by_y)
    s_a, m_0 = together(s_a, m_0)
    s_b, s_a = together(s_b, s_a)
    s_c = send(s_b, outer)
    m_a, m_b = send(s_a, by_core), send(s_b, by_core)
    m_a, m_b, x_0, y_1 = together(m_a, m_b, x_0, y_1)
    d_0 = send(x_0, by_y)
    d_1 = across(y_1)
    x_1, y_0 = together(x_1, y_0)
    mine = (own[0], x_0, own[1], x_1)
    u_0, v_0, u_a, v_a, u_b, v_b = run((s_0, m_0, s_a, m_a, s_b, m_b), [(0, mine, 0, 6)], [None] * 6)
    s_c, u_0, v_0, u_a, v_a, u_b, v_b = together(s_c, u_0, v_0, u_a, v_a, u_b, v_b)
    m_c = send(s_c, by_core)
    (m_c,) = together(m_c)
    u_c, v_c = run((s_c, m_c), [(0, mine, 0, 2)], [None] * 2)
    d_0, d_1, u_c, v_c = together(d_0, d_1, u_c, v_c)
    theirs = (y_0, d_0, y_1, d_1)
    p_c, o_c = run((s_c, m_c), [(1, theirs, 0, 2)], [u_c, v_c])
    r_c = send(o_c, by_core)

    r_c, p_c = together(r_c, p_c)
    r_n = send(add(p_c, r_c), outer)
    p_b, o_b, p_a, o_a, p_0, o_0 = run((s_b, m_b, s_a, m_a, s_0, m_0), [(1, theirs, 0, 6)], [u_b, v_b, u_a, v_a, u_0, v_0])
    r_b, r_a, r_0 = send(o_b, by_core), send(o_a, by_core), send(o_0, by_core)
    r_n, p_a = lax.optimization_barrier((r_n, p_a))
    r_b, r_a, p_b, r_n = lax.optimization_barrier((r_b, r_a, p_b, r_n))
    r_o = send(add(p_a, r_a), outer)
    r_m = send(add(p_b, r_b, r_n), skip)
    order[0] = p_0
    (r_m,) = together(r_m)
    (r_o,) = together(r_o)
    return add(tokens, order[0], r_0, r_o, r_m)


def solution(mesh):
    placed = (
        P(("dp", "tensor"), None),
        P("dp"),
        P(("dp", "tensor"), None),
        P(),
        P(),
        P("tensor", "dp", None),
        P("tensor", "dp", None),
        P("tensor", None, "dp"),
    )

    def shards(*args):
        fits = mesh.shape["dp"] == 2 and mesh.shape["tensor"] == 16 and args[5].shape[0] == 1
        fits = fits and args[1].shape[0] == 1 and args[0].shape[0] == 256 and args[4].shape[1] == GATE_ROWS
        fits = fits and args[5].shape[2] == 512 and args[0].shape[1] == 1536
        return (lanes if fits else general)(*args)

    return jax.shard_map(
        shards, mesh=mesh, in_specs=placed, out_specs=P(("dp", "tensor"), None), check_vma=False
    )
```
